256 devices in a mesh: depth: 128 (over x, y, z_lo, core), lat: 2 (over z_hi).
Axes of the slice: x: 4, y: 4, z: 8 (z_hi: 2, z_lo: 4; z = z_hi * 4 + z_lo), core: 2. Of those that a mesh axis runs over, the one named last changes fastest.
Arguments:
- sources: float32 [128, 16, 6144], P('depth', None, 'lat'), may hold values from -6 to 6
- frontal: bfloat16 [128, 48, 8, 128, 128], P('depth', 'lat'), may hold values from -0.1875 to 0.1875
- couplings: bfloat16 [128, 2, 48, 2, 128, 128], P('depth', None, 'lat'), may hold values from -0.375 to 0.375
- pattern: int32 [128, 48, 8], P('depth', 'lat'), may hold values from 0 to 47, as said below
Outputs:
- swept: float32 [128, 16, 6144], P('depth', None, 'lat')
The draws below stay inside these ranges and needn't reach their ends.
Inputs may be any that keep to these rules, and one draw needn't show every extreme that they name: Entry 0 of pattern[p, r] is r itself; the other entries of a block row differ from r and from each other.
All inputs are finite; a program needn't handle non-finite values.
Results may differ from the reference program's by a relative error of at most 0.035.
Values may be sent and summed in bfloat16 or wider, within the bound.
A program may use at most 128 MiB of HBM per device.

```python
import jax
import jax.numpy as jnp
from jax import lax

BLK = 128
KH = 8
KC = 2
SEG = 8
SHOTS = 16
UNK = 6144
NBR = 48
PANELS = 128


def draw_pattern(key, part):
    key = jax.random.fold_in(key, 11)
    keys = jax.random.split(key, PANELS * NBR)
    offsets = jax.vmap(lambda single: jax.random.permutation(single, NBR - 1)[:KH - 1])(keys)
    rows = jnp.arange(PANELS * NBR, dtype=jnp.int32) % NBR
    others = (rows[:, None] + 1 + offsets.astype(jnp.int32)) % NBR
    joined = jnp.concatenate([rows[:, None], others], axis=1)
    return joined.reshape(PANELS, NBR, KH).astype(jnp.int32)


def block_scale(rng, extent, cuts, smallest, top_value):
    def one(axis_at, parts):
        draws = jax.random.uniform(jax.random.fold_in(jax.random.fold_in(rng, 6), axis_at), (parts,), jnp.float32, smallest / len(cuts), top_value / len(cuts))
        return jnp.repeat(jnp.exp(draws), extent[axis_at] // parts).reshape((-1,) + (1,) * (len(extent) - axis_at - 1))

    loudness = one(*cuts[0])
    for cut in cuts[1:]:
        loudness = loudness * one(*cut)
    return loudness


def scatter_about(rng, dims, scale, bound, pieces=(), kind=jnp.bfloat16):
    values = scale * jax.random.normal(rng, dims, jnp.float32)
    if pieces:
        values = values * block_scale(rng, dims, pieces, -0.22, 0.18)
    return jnp.clip(values, -bound, bound).astype(kind)


def setup_inputs(seed: int = 0) -> dict:
    key_of = jax.random.split(jax.random.key(seed), 5)
    return {
        "sources": scatter_about(key_of[0], (PANELS, SHOTS, UNK), 1.0, 6.0, ((0, 128), (2, 2)), jnp.float32),
        "frontal": scatter_about(key_of[1], (PANELS, NBR, KH, BLK, BLK), (KH * BLK) ** -0.5, 0.1875, ((0, 128), (1, 2))),
        "couplings": scatter_about(key_of[2], (PANELS, 2, NBR, KC, BLK, BLK), (KC * BLK) ** -0.5, 0.375, ((0, 128), (2, 2))),
        "pattern": draw_pattern(jax.random.fold_in(key_of[4], 71), 0),
    }


def apply_blocks(blocks, cols, vector):
    shots = vector.shape[0]
    grouped = vector.reshape(shots, NBR, BLK)
    picked = grouped[:, cols]
    result = jnp.einsum("rkij,srkj->sri", blocks.astype(jnp.float32), picked.astype(jnp.float32))
    return result.reshape(shots, UNK)


def reference(sources, frontal, couplings, pattern):
    places = jnp.arange(PANELS, dtype=jnp.int32)

    def forward_step(prior, inputs):
        source, factor, coupling, cols, place = inputs
        prior = jnp.where(place % SEG == 0, jnp.zeros_like(prior), prior)
        coupled = apply_blocks(coupling[0], cols[:, :KC], prior)
        reduced = (source - coupled).astype(jnp.bfloat16)
        field = apply_blocks(factor, cols, reduced)
        return field.astype(jnp.bfloat16), field

    start = jnp.zeros((SHOTS, UNK), jnp.bfloat16)
    _, forward = lax.scan(forward_step, start, (sources, frontal, couplings, pattern, places))

    def backward_step(later, inputs):
        field, factor, coupling, cols, place = inputs
        later = jnp.where(place % SEG == SEG - 1, jnp.zeros_like(later), later)
        pulled = apply_blocks(coupling[1], cols[:, :KC], later).astype(jnp.bfloat16)
        swept = field - apply_blocks(factor, cols, pulled)
        return swept.astype(jnp.bfloat16), swept

    _, swept = lax.scan(backward_step, start, (forward, frontal, couplings, pattern, places), reverse=True)
    return swept
```

```python
import functools

import jax
import jax.numpy as jnp
from jax import lax
from jax.experimental import pallas as pl
from jax.experimental.pallas import tpu as pltpu
from jax.sharding import PartitionSpec as P

MESH = pl.DeviceIdType.MESH
BLK = 128
KH = 8
KC = 2
SEG = 8
SHOTS = 16
NBR = 48
HALF = 24
CHUNKS = 4
ROWS = HALF // CHUNKS
F32 = jnp.float32
BF16 = jnp.bfloat16
NN = (((1,), (0,)), ((), ()))
NT = (((1,), (1,)), ((), ()))


def gathered(vector, cols, row, count):
    return jnp.concatenate([vector[cols[row, k]] for k in range(count)], axis=1)


def row_apply(blocks, vector, cols, row, count):
    operand = gathered(vector, cols, row, count)
    weights = blocks[row].reshape(count * BLK, BLK)
    return lax.dot_general(operand, weights, NN, preferred_element_type=F32)


def row_apply_plain(blocks, vector, cols, row, count):
    operand = gathered(vector, cols, row, count)
    weights = jnp.concatenate([blocks[row, k] for k in range(count)], axis=1)
    return lax.dot_general(operand, weights, NT, preferred_element_type=F32)


def transpose_blocks(blocks, rows, count):
    def one(row, carry):
        for k in range(count):
            blocks[row, k] = blocks[row, k].T
        return carry

    lax.fori_loop(0, rows, one, 0, unroll=2)


def sweep_kernel(
    sources, frontal, couplings, cols, swept,
    factor, ahead, behind, field, incoming, later, reduced, pulled, out_fwd, out_bwd,
    load_sem, lat_send, lat_recv, fwd_send, fwd_recv, bwd_send, bwd_recv,
):
    depth = lax.axis_index("depth")
    half = lax.axis_index("lat")
    place = lax.rem(depth, SEG)
    other = 1 - half
    base = half * HALF

    load_factor = pltpu.make_async_copy(frontal, factor, load_sem.at[0])
    load_ahead = pltpu.make_async_copy(couplings.at[0], ahead, load_sem.at[1])
    load_behind = pltpu.make_async_copy(couplings.at[1], behind, load_sem.at[2])
    load_factor.start()
    load_ahead.start()
    load_behind.start()

    barrier = pltpu.get_barrier_semaphore()
    pl.semaphore_signal(barrier, inc=1, device_id=(depth, other), device_id_type=MESH)

    @pl.when(place > 0)
    def _():
        for lat in range(2):
            pl.semaphore_signal(barrier, inc=1, device_id=(depth - 1, lat), device_id_type=MESH)

    @pl.when(place < SEG - 1)
    def _():
        for lat in range(2):
            pl.semaphore_signal(barrier, inc=1, device_id=(depth + 1, lat), device_id_type=MESH)

    at_edge = jnp.logical_or(place == 0, place == SEG - 1)
    pl.semaphore_wait(barrier, jnp.where(at_edge, 3, 5))

    def across(vector, slot):
        mine = vector.at[pl.ds(base, HALF)]
        return pltpu.make_async_remote_copy(
            src_ref=mine, dst_ref=mine, send_sem=lat_send.at[slot], recv_sem=lat_recv.at[slot],
            device_id=(depth, other), device_id_type=MESH,
        )

    def arriving_across(vector, slot):
        theirs = vector.at[pl.ds(other * HALF, HALF)]
        return pltpu.make_async_remote_copy(
            src_ref=theirs, dst_ref=theirs, send_sem=lat_send.at[slot], recv_sem=lat_recv.at[slot],
            device_id=(depth, other), device_id_type=MESH,
        )

    def chunk_copy(source, target, chunk, far, owner, step, send, recv):
        lat = other if far else half
        return pltpu.make_async_remote_copy(
            src_ref=source.at[pl.ds(chunk * ROWS, ROWS)],
            dst_ref=target.at[pl.ds(owner * HALF + chunk * ROWS, ROWS)],
            send_sem=send.at[far, chunk], recv_sem=recv.at[far, chunk],
            device_id=(depth + step, lat), device_id_type=MESH,
        )

    def forward_copy(chunk, far, owner):
        return chunk_copy(out_fwd, incoming, chunk, far, owner, 1, fwd_send, fwd_recv)

    def backward_copy(chunk, far, owner):
        return chunk_copy(out_bwd, later, chunk, far, owner, -1, bwd_send, bwd_recv)

    def wait_arrivals(make):
        for far in range(2):
            owner = other if far else half
            for chunk in range(CHUNKS):
                make(chunk, far, owner).wait_recv()

    def start_chunk(make, chunk):
        for far in (1, 0):
            make(chunk, far, half).start()

    def wait_sent(make):
        for far in range(2):
            for chunk in range(CHUNKS):
                make(chunk, far, half).wait_send()

    @pl.when(place == 0)
    def _():
        for row in range(HALF):
            reduced[base + row] = sources[:, row * BLK:(row + 1) * BLK].astype(BF16)

    @pl.when(place > 0)
    def _():
        load_ahead.wait()
        transpose_blocks(ahead, HALF, KC)
        load_factor.wait()
        transpose_blocks(factor, HALF, KH)
        wait_arrivals(forward_copy)
        for row in range(HALF):
            coupled = row_apply(ahead, incoming, cols, row, KC)
            reduced[base + row] = (sources[:, row * BLK:(row + 1) * BLK] - coupled).astype(BF16)

    send_reduced = across(reduced, 0)
    send_reduced.start()
    arriving_across(reduced, 0).wait_recv()

    @pl.when(place == 0)
    def _():
        load_ahead.wait()
        load_factor.wait()
        for chunk in range(CHUNKS):
            for row in range(chunk * ROWS, (chunk + 1) * ROWS):
                value = row_apply_plain(factor, reduced, cols, row, KH)
                field[row] = value
                out_fwd[row] = value.astype(BF16)
            start_chunk(forward_copy, chunk)
        transpose_blocks(factor, HALF, KH)

    @pl.when(place > 0)
    def _():
        for chunk in range(CHUNKS):
            for row in range(chunk * ROWS, (chunk + 1) * ROWS):
                value = row_apply(factor, reduced, cols, row, KH)
                field[row] = value
                out_fwd[row] = value.astype(BF16)

            @pl.when(place < SEG - 1)
            def _():
                start_chunk(forward_copy, chunk)

            @pl.when(place == SEG - 1)
            def _():
                for row in range(chunk * ROWS, (chunk + 1) * ROWS):
                    out_bwd[row] = out_fwd[row]
                start_chunk(backward_copy, chunk)

    load_behind.wait()

    @pl.when(place == SEG - 1)
    def _():
        for row in range(HALF):
            swept[:, row * BLK:(row + 1) * BLK] = field[row]

    @pl.when(place < SEG - 1)
    def _():
        transpose_blocks(behind, HALF, KC)
        wait_arrivals(backward_copy)
        for row in range(HALF):
            pulled[base + row] = row_apply(behind, later, cols, row, KC).astype(BF16)
        send_pulled = across(pulled, 1)
        send_pulled.start()
        arriving_across(pulled, 1).wait_recv()
        for chunk in range(CHUNKS):
            for row in range(chunk * ROWS, (chunk + 1) * ROWS):
                value = field[row] - row_apply(factor, pulled, cols, row, KH)
                swept[:, row * BLK:(row + 1) * BLK] = value
                out_bwd[row] = value.astype(BF16)

            @pl.when(place > 0)
            def _():
                start_chunk(backward_copy, chunk)

        send_pulled.wait_send()
        wait_sent(forward_copy)

    @pl.when(place > 0)
    def _():
        wait_sent(backward_copy)

    send_reduced.wait_send()


def local(sources, frontal, couplings, pattern):
    vector = pltpu.VMEM((NBR, SHOTS, BLK), BF16)
    half_vector = pltpu.VMEM((HALF, SHOTS, BLK), BF16)
    vmem = pl.BlockSpec(memory_space=pltpu.VMEM)
    hbm = pl.BlockSpec(memory_space=pl.ANY)
    smem = pl.BlockSpec(memory_space=pltpu.SMEM)
    out = pl.pallas_call(
        sweep_kernel,
        out_shape=jax.ShapeDtypeStruct((SHOTS, HALF * BLK), F32),
        in_specs=[vmem, hbm, hbm, smem],
        out_specs=vmem,
        scratch_shapes=[
            pltpu.VMEM((HALF, KH, BLK, BLK), BF16),
            pltpu.VMEM((HALF, KC, BLK, BLK), BF16),
            pltpu.VMEM((HALF, KC, BLK, BLK), BF16),
            pltpu.VMEM((HALF, SHOTS, BLK), F32),
            vector, vector, vector, vector, half_vector, half_vector,
            pltpu.SemaphoreType.DMA((3,)),
            pltpu.SemaphoreType.DMA((2,)),
            pltpu.SemaphoreType.DMA((2,)),
            pltpu.SemaphoreType.DMA((2, CHUNKS)),
            pltpu.SemaphoreType.DMA((2, CHUNKS)),
            pltpu.SemaphoreType.DMA((2, CHUNKS)),
            pltpu.SemaphoreType.DMA((2, CHUNKS)),
        ],
        compiler_params=pltpu.CompilerParams(
            collective_id=0, has_side_effects=True, vmem_limit_bytes=48 * 1024 * 1024
        ),
    )(sources[0], frontal[0], couplings[0], pattern[0])
    return out[None]


def solution(mesh):
    return jax.shard_map(
        local,
        mesh=mesh,
        in_specs=(
            P("depth", None, "lat"),
            P("depth", "lat", None, None, None),
            P("depth", None, "lat", None, None, None),
            P("depth", "lat", None),
        ),
        out_specs=P("depth", None, "lat"),
        check_vma=False,
    )
```

```python
import jax
import jax.numpy as jnp
from jax import lax
from jax.experimental import pallas as pl
from jax.experimental.pallas import tpu as pltpu
from jax.sharding import PartitionSpec as P

MESH = pl.DeviceIdType.MESH
BLK = 128
KH = 8
KC = 2
SEG = 8
SHOTS = 16
NBR = 48
HALF = 24
CHUNKS = 4
ROWS = HALF // CHUNKS
F32 = jnp.float32
BF16 = jnp.bfloat16
NN = (((1,), (0,)), ((), ()))

SWAP_AHEAD = (2,)
SWAP_BEHIND = ()
AHEAD, BEHIND = range(2)
AFTER_START = ()
AT_FORWARD = ((0, 4, AHEAD), (1, 5, AHEAD), (1, 6, AHEAD), (2, 7, AHEAD), (6, 1, BEHIND))
AT_BACKWARD = ((6, 2, BEHIND),)
PACE_AHEAD = (0, 24, 0, 24, 2, 2, 2, 2)
PACE_BEHIND = (12, 3, 4, 12, 3, 4, 24, 0)
FIRST_AHEAD = (1, 3)
FIRST_BEHIND = (6,)
PACES = (PACE_AHEAD, PACE_BEHIND)
AFTER_START = tuple(told for told in AFTER_START if PACES[told[2]][told[1]])
AT_FORWARD = tuple(told for told in AT_FORWARD if PACES[told[2]][told[1]])
AT_BACKWARD = tuple(told for told in AT_BACKWARD if PACES[told[2]][told[1]])
TOLD = AFTER_START + AT_FORWARD + AT_BACKWARD
GREETS = tuple(sorted({(min(i, j), max(i, j)) for i, j, _ in TOLD if abs(i - j) > 1}))


def any_of(place, places):
    found = place < 0
    for one in places:
        found = jnp.logical_or(found, place == one)
    return found


def dot(operand, weights):
    return lax.dot_general(operand, weights, NN, preferred_element_type=F32)


def gathered(vector, cols, row, count):
    return jnp.concatenate([vector[cols[k, row]] for k in range(count)], axis=1)


def row_apply(blocks, vector, cols, row):
    return dot(gathered(vector, cols, row, KH), blocks[row].reshape(KH * BLK, BLK))


def transpose_factor(blocks):
    def one(row, carry):
        for k in range(KH):
            blocks[row, k] = blocks[row, k].T
        return carry

    lax.fori_loop(0, HALF, one, 0, unroll=2)


def split_couplings(raw, diagonal, beside, base):
    def one(row, carry):
        diagonal[row] = raw[row, 0].T
        beside[base + row] = raw[row, 1].T
        return carry

    lax.fori_loop(0, HALF, one, 0, unroll=4)


def sweep_kernel(
    sources_hbm, frontal, couplings, pattern, cols, swept,
    sources, partial, factor, raw, diag_ahead, diag_behind, side_ahead, side_behind, diag_next, diag_prior,
    rounded, source_next, their_pattern, their_cols, field, incoming, later, incoming_plus, later_plus, reduced, pulled, out_fwd, out_bwd,
    load_sem, once_send, once_recv, fwd_send, fwd_recv, bwd_send, bwd_recv, go,
):
    depth = lax.axis_index("depth")
    half = lax.axis_index("lat")
    place = lax.rem(depth, SEG)
    other = 1 - half
    base = half * HALF
    their_base = other * HALF

    load_factor = pltpu.make_async_copy(frontal, factor, load_sem.at[0])
    load_ahead = pltpu.make_async_copy(couplings.at[0], raw.at[0], load_sem.at[1])
    load_behind = pltpu.make_async_copy(couplings.at[1], raw.at[1], load_sem.at[2])
    load_sources = pltpu.make_async_copy(sources_hbm, sources, load_sem.at[4])
    load_sources.start()
    load_ahead.start()
    load_factor.start()
    load_behind.start()

    barrier = pltpu.get_barrier_semaphore()

    def greet(depth_index, lat):
        pl.semaphore_signal(barrier, inc=1, device_id=(depth_index, lat), device_id_type=MESH)

    greet(depth, other)

    @pl.when(place > 0)
    def _():
        greet(depth - 1, half)
        greet(depth - 1, other)

    @pl.when(place < SEG - 1)
    def _():
        greet(depth + 1, half)
        greet(depth + 1, other)

    for one, two in GREETS:
        @pl.when(place == one)
        def _():
            greet(depth + (two - one), half)

        @pl.when(place == two)
        def _():
            greet(depth - (two - one), half)

    at_edge = jnp.logical_or(place == 0, place == SEG - 1)
    callers = jnp.where(at_edge, 3, 5)
    for pair in GREETS:
        callers = callers + jnp.where(any_of(place, pair), 1, 0)

    load_sources.wait()
    load_ahead.wait()

    @pl.when(place == 0)
    def _():
        for row in range(HALF):
            reduced[base + row] = sources[:, row * BLK:(row + 1) * BLK].astype(BF16)

    @pl.when(place > 0)
    def _():
        split_couplings(raw.at[0], diag_ahead, side_ahead, base)
        for row in range(HALF):
            rounded[row] = sources[:, row * BLK:(row + 1) * BLK].astype(BF16)

    pl.semaphore_wait(barrier, callers)

    def tell(table):
        for one, two, slot in table:
            @pl.when(place == one)
            def _():
                pl.semaphore_signal(
                    go.at[slot], inc=1, device_id=(depth + (two - one), half), device_id_type=MESH
                )

    def wait_told(slot, among):
        places = [two for _, two, kind in TOLD if kind == slot and two in among]

        @pl.when(any_of(place, places))
        def _():
            pl.semaphore_wait(go.at[slot], 1)

    def once(source, target, slot, step, lat):
        return pltpu.make_async_remote_copy(
            src_ref=source, dst_ref=target, send_sem=once_send.at[slot], recv_sem=once_recv.at[slot],
            device_id=(depth + step, lat), device_id_type=MESH,
        )

    mine = pl.ds(base, HALF)
    theirs = pl.ds(their_base, HALF)
    swaps_ahead = any_of(place, SWAP_AHEAD)
    swaps_behind = any_of(place, SWAP_BEHIND)
    ahead_swaps = any_of(place + 1, SWAP_AHEAD)
    behind_swaps = any_of(place - 1, SWAP_BEHIND)
    give_reduced = once(reduced.at[mine], reduced.at[mine], 0, 0, other)
    take_reduced = once(reduced.at[theirs], reduced.at[theirs], 0, 0, other)
    give_pulled = once(pulled.at[mine], pulled.at[mine], 7, 0, other)
    take_pulled = once(pulled.at[theirs], pulled.at[theirs], 7, 0, other)
    give_pattern = once(pattern, their_pattern, 1, 0, other)
    give_source = once(rounded, source_next, 2, -1, half)
    give_diag_ahead = once(diag_ahead, diag_next, 3, -1, half)
    give_diag_behind = once(diag_behind, diag_prior, 4, 1, half)

    def side_copy(blocks, kind, owner, first, rows):
        part = blocks.at[pl.ds(owner * HALF + first, rows)]
        return once(part, part, 5 + kind, 0, other)

    def give_side(blocks, kind, paces, places, first=lambda: None):
        for pace in sorted(set(paces[p] for p in places if paces[p])):
            group = [p for p in places if paces[p] == pace]

            @pl.when(any_of(place, group))
            def _():
                wait_told(kind, group)
                first()

                def part(step, carry):
                    copy = side_copy(blocks, kind, half, step * pace, pace)
                    copy.start()
                    copy.wait_send()
                    return carry

                lax.fori_loop(0, HALF // pace, part, 0)

    def take_side(blocks, kind):
        side_copy(blocks, kind, other, 0, HALF).wait_recv()

    def chunk_copy(source, target, chunk, kind, owner, step, send, recv):
        return pltpu.make_async_remote_copy(
            src_ref=source.at[kind // 2, pl.ds(chunk * ROWS, ROWS)],
            dst_ref=target.at[pl.ds(owner * HALF + chunk * ROWS, ROWS)],
            send_sem=send.at[kind, chunk], recv_sem=recv.at[kind, chunk],
            device_id=(depth + step, other if kind else half), device_id_type=MESH,
        )

    def forward_copy(chunk, kind, owner):
        return chunk_copy(out_fwd, incoming_plus if kind == 2 else incoming, chunk, kind, owner, 1, fwd_send, fwd_recv)

    def backward_copy(chunk, kind, owner):
        return chunk_copy(out_bwd, later_plus if kind == 2 else later, chunk, kind, owner, -1, bwd_send, bwd_recv)

    def wait_arrivals(make, kinds):
        for kind in kinds:
            for chunk in range(CHUNKS):
                make(chunk, kind, other if kind else half).wait_recv()

    def wait_sent(make, swaps):
        for kind in (0, 1):
            for chunk in range(CHUNKS):
                make(chunk, kind, half).wait_send()

        @pl.when(jnp.logical_not(swaps))
        def _():
            for chunk in range(CHUNKS):
                make(chunk, 2, half).wait_send()

    def in_chunks(make, out, compute, ahead_of, swaps):
        for chunk in range(CHUNKS + 1):
            if chunk < CHUNKS:
                for row in range(chunk * ROWS, (chunk + 1) * ROWS):
                    out[0, row] = compute(row).astype(BF16)
                make(chunk, 1, half).start()
                make(chunk, 0, half).start()
            if chunk > 0:
                for row in range((chunk - 1) * ROWS, chunk * ROWS):
                    out[1, row] = ahead_of(out[0, row], row).astype(BF16)

                @pl.when(jnp.logical_not(swaps))
                def _():
                    make(chunk - 1, 2, half).start()

    def next_source(sent, row):
        return source_next[row] - dot(sent, diag_next[row])

    def prior_pulled(sent, row):
        return dot(sent, diag_prior[row])

    @pl.when(place == 0)
    def _():
        give_reduced.start()
        give_reduced.wait_send()

    tell(AFTER_START)
    give_pattern.start()

    @pl.when(jnp.logical_and(place > 0, jnp.logical_not(swaps_ahead)))
    def _():
        give_source.start()
        give_diag_ahead.start()

    give_side(side_ahead, AHEAD, PACE_AHEAD, FIRST_AHEAD)

    load_behind.wait()

    def take_diag_prior():
        @pl.when(jnp.logical_not(behind_swaps))
        def _():
            give_diag_behind.wait_recv()

    def prepare_behind():
        split_couplings(raw.at[1], diag_behind, side_behind, base)

    def start_diag_behind():
        @pl.when(jnp.logical_not(swaps_behind))
        def _():
            give_diag_behind.start()

    @pl.when(place < SEG - 1)
    def _():
        prepare_behind()

        @pl.when(lax.rem(place, 2) == 0)
        def _():
            start_diag_behind()

    give_side(side_behind, BEHIND, PACE_BEHIND, FIRST_BEHIND)
    load_factor.wait()
    transpose_factor(factor)

    give_side(side_ahead, AHEAD, PACE_AHEAD, [p for p in range(1, SEG) if p not in FIRST_AHEAD])
    give_pattern.wait_recv()
    load_cols = pltpu.make_async_copy(their_pattern, their_cols, load_sem.at[3])
    load_cols.start()
    load_cols.wait()

    @pl.when(place == 0)
    def _():
        take_reduced.wait_recv()

    def forward_row(row):
        value = row_apply(factor, reduced, cols, row)
        field[row] = value
        return value

    def last_row(row):
        value = row_apply(factor, reduced, cols, row)
        swept[:, row * BLK:(row + 1) * BLK] = value
        return value

    def backward_row(row):
        value = field[row] - row_apply(factor, pulled, cols, row)
        swept[:, row * BLK:(row + 1) * BLK] = value
        return value

    @pl.when(place > 0)
    def _():
        wait_arrivals(forward_copy, (0,))
        for row in range(HALF):
            near = dot(incoming[base + row], diag_ahead[row])
            partial[row] = sources[:, row * BLK:(row + 1) * BLK] - near
        wait_arrivals(forward_copy, (1,))
        for row in range(HALF):
            beside = dot(incoming[cols[1, row]], side_ahead[base + row])
            reduced[base + row] = (partial[row] - beside).astype(BF16)

        @pl.when(swaps_ahead)
        def _():
            give_reduced.start()
            take_reduced.wait_recv()

        @pl.when(jnp.logical_not(swaps_ahead))
        def _():
            take_side(side_ahead, AHEAD)
            wait_arrivals(forward_copy, (2,))
            for row in range(HALF):
                beside = dot(incoming[their_cols[1, row]], side_ahead[their_base + row])
                reduced[their_base + row] = (incoming_plus[their_base + row] - beside).astype(BF16)

    @pl.when(jnp.logical_and(place < SEG - 1, jnp.logical_not(ahead_swaps)))
    def _():
        give_source.wait_recv()
        give_diag_ahead.wait_recv()

    @pl.when(place == SEG - 1)
    def _():
        take_diag_prior()
        in_chunks(backward_copy, out_bwd, last_row, prior_pulled, behind_swaps)

    @pl.when(place < SEG - 1)
    def _():
        in_chunks(forward_copy, out_fwd, forward_row, next_source, ahead_swaps)

    tell(AT_FORWARD)

    @pl.when(place == 3)
    def _():
        start_diag_behind()

    def start_diag_far():
        @pl.when(any_of(place, (1, 5)))
        def _():
            start_diag_behind()


    rest = [p for p in range(SEG - 1) if p not in FIRST_BEHIND]
    give_side(side_behind, BEHIND, PACE_BEHIND, rest, start_diag_far)

    @pl.when(place < SEG - 1)
    def _():
        wait_sent(forward_copy, ahead_swaps)

    @pl.when(place < SEG - 1)
    def _():
        wait_arrivals(backward_copy, (0,))
        for row in range(HALF):
            partial[row] = dot(later[base + row], diag_behind[row])
        wait_arrivals(backward_copy, (1,))
        for row in range(HALF):
            beside = dot(later[cols[1, row]], side_behind[base + row])
            pulled[base + row] = (partial[row] + beside).astype(BF16)

        @pl.when(swaps_behind)
        def _():
            give_pulled.start()
            take_pulled.wait_recv()

        @pl.when(jnp.logical_not(swaps_behind))
        def _():
            take_side(side_behind, BEHIND)
            wait_arrivals(backward_copy, (2,))
            for row in range(HALF):
                beside = dot(later[their_cols[1, row]], side_behind[their_base + row])
                pulled[their_base + row] = (later_plus[their_base + row] + beside).astype(BF16)

        @pl.when(place > 0)
        def _():
            take_diag_prior()
            in_chunks(backward_copy, out_bwd, backward_row, prior_pulled, behind_swaps)

        @pl.when(place == 0)
        def _():
            for row in range(HALF):
                backward_row(row)


    tell(AT_BACKWARD)

    @pl.when(place > 0)
    def _():
        wait_sent(backward_copy, behind_swaps)

    @pl.when(swaps_ahead)
    def _():
        give_reduced.wait_send()

    @pl.when(swaps_behind)
    def _():
        give_pulled.wait_send()

    give_pattern.wait_send()

    @pl.when(jnp.logical_and(place > 0, jnp.logical_not(swaps_ahead)))
    def _():
        give_source.wait_send()
        give_diag_ahead.wait_send()

    @pl.when(jnp.logical_and(place < SEG - 1, jnp.logical_not(swaps_behind)))
    def _():
        give_diag_behind.wait_send()


def local(sources, frontal, couplings, pattern):
    vector = pltpu.VMEM((NBR, SHOTS, BLK), BF16)
    half_vector = pltpu.VMEM((HALF, SHOTS, BLK), BF16)
    half_double = pltpu.VMEM((2, HALF, SHOTS, BLK), BF16)
    half_blocks = pltpu.VMEM((HALF, BLK, BLK), BF16)
    blocks = pltpu.VMEM((NBR, BLK, BLK), BF16)
    vmem = pl.BlockSpec(memory_space=pltpu.VMEM)
    hbm = pl.BlockSpec(memory_space=pl.ANY)
    smem = pl.BlockSpec(memory_space=pltpu.SMEM)
    chunk_sem = pltpu.SemaphoreType.DMA((3, CHUNKS))
    columns = pattern[0].T
    once_sem = pltpu.SemaphoreType.DMA((8,))
    out = pl.pallas_call(
        sweep_kernel,
        out_shape=jax.ShapeDtypeStruct((SHOTS, HALF * BLK), F32),
        in_specs=[hbm, hbm, hbm, hbm, smem],
        out_specs=vmem,
        scratch_shapes=[
            pltpu.VMEM((SHOTS, HALF * BLK), F32),
            pltpu.VMEM((HALF, SHOTS, BLK), F32),
            pltpu.VMEM((HALF, KH, BLK, BLK), BF16),
            pltpu.VMEM((2, HALF, KC, BLK, BLK), BF16),
            half_blocks, half_blocks, blocks, blocks, half_blocks, half_blocks,
            half_vector, half_vector,
            pltpu.VMEM((KH, HALF), jnp.int32),
            pltpu.SMEM((KH, HALF), jnp.int32),
            pltpu.VMEM((HALF, SHOTS, BLK), F32),
            vector, vector, vector, vector, vector, vector, half_double, half_double,
            pltpu.SemaphoreType.DMA((5,)),
            once_sem, once_sem, chunk_sem, chunk_sem, chunk_sem, chunk_sem,
            pltpu.SemaphoreType.REGULAR((2,)),
        ],
        compiler_params=pltpu.CompilerParams(
            collective_id=0, has_side_effects=True, vmem_limit_bytes=60 * 1024 * 1024
        ),
    )(sources[0], frontal[0], couplings[0], columns, columns)
    return out[None]


def solution(mesh):
    return jax.shard_map(
        local,
        mesh=mesh,
        in_specs=(
            P("depth", None, "lat"),
            P("depth", "lat", None, None, None),
            P("depth", None, "lat", None, None, None),
            P("depth", "lat", None),
        ),
        out_specs=P("depth", None, "lat"),
        check_vma=False,
    )
```

```python
import jax
import jax.numpy as jnp
from jax import lax
from jax.experimental import pallas as pl
from jax.experimental.pallas import tpu as pltpu
from jax.sharding import PartitionSpec as P

MESH = pl.DeviceIdType.MESH
BLK = 128
KH = 8
KC = 2
SEG = 8
SHOTS = 16
NBR = 48
HALF = 24
CHUNKS = 3
ROWS = HALF // CHUNKS
F32 = jnp.float32
BF16 = jnp.bfloat16
NN = (((1,), (0,)), ((), ()))

SWAP_AHEAD = (2,)
SWAP_BEHIND = (6,)
AHEAD, BEHIND = range(2)
AFTER_START = ()
AT_FORWARD = ((0, 4, AHEAD), (1, 5, AHEAD), (3, 7, AHEAD), (7, 1, BEHIND))
AT_BACKWARD = ((6, 2, BEHIND), (6, 3, BEHIND))
PACE_AHEAD = (0, 24, 0, 24, 2, 2, 24, 4)
PACE_BEHIND = (4, 4, 4, 8, 3, 4, 0, 0)
FIRST_AHEAD = (1, 3, 6)
PACES = (PACE_AHEAD, PACE_BEHIND)
AFTER_START = tuple(told for told in AFTER_START if PACES[told[2]][told[1]])
AT_FORWARD = tuple(told for told in AT_FORWARD if PACES[told[2]][told[1]])
AT_BACKWARD = tuple(told for told in AT_BACKWARD if PACES[told[2]][told[1]])
TOLD = AFTER_START + AT_FORWARD + AT_BACKWARD
GREETS = tuple(sorted({(min(i, j), max(i, j)) for i, j, _ in TOLD if abs(i - j) > 1}))


def any_of(place, places):
    found = place < 0
    for one in places:
        found = jnp.logical_or(found, place == one)
    return found


def dot(operand, weights):
    return lax.dot_general(operand, weights, NN, preferred_element_type=F32)


def gathered(vector, cols, row, count):
    return jnp.concatenate([vector[cols[k, row]] for k in range(count)], axis=1)


def row_apply(blocks, vector, cols, row):
    return dot(gathered(vector, cols, row, KH), blocks[row].reshape(KH * BLK, BLK))


def transpose_factor(blocks):
    def one(row, carry):
        for k in range(KH):
            blocks[row, k] = blocks[row, k].T
        return carry

    lax.fori_loop(0, HALF, one, 0, unroll=2)


def split_couplings(raw, diagonal, beside, base):
    def one(row, carry):
        diagonal[row] = raw[row, 0].T
        beside[base + row] = raw[row, 1].T
        return carry

    lax.fori_loop(0, HALF, one, 0, unroll=4)


def sweep_kernel(
    sources_hbm, frontal, couplings, pattern, cols, swept,
    sources, partial, theirs_part, factor, raw, diag_ahead, diag_behind, side_ahead, side_behind, diag_next, diag_prior,
    rounded, source_next, their_pattern, their_cols, field, incoming, later, incoming_plus, later_plus, reduced, pulled, out_fwd, out_bwd,
    load_sem, once_send, once_recv, fwd_send, fwd_recv, bwd_send, bwd_recv, go,
):
    depth = lax.axis_index("depth")
    half = lax.axis_index("lat")
    place = lax.rem(depth, SEG)
    other = 1 - half
    base = half * HALF
    their_base = other * HALF

    load_factor = pltpu.make_async_copy(frontal, factor, load_sem.at[0])
    load_ahead = pltpu.make_async_copy(couplings.at[0], raw.at[0], load_sem.at[1])
    load_behind = pltpu.make_async_copy(couplings.at[1], raw.at[1], load_sem.at[2])
    load_sources = pltpu.make_async_copy(sources_hbm, sources, load_sem.at[4])
    load_sources.start()
    load_ahead.start()
    load_factor.start()
    load_behind.start()

    barrier = pltpu.get_barrier_semaphore()

    def greet(depth_index, lat):
        pl.semaphore_signal(barrier, inc=1, device_id=(depth_index, lat), device_id_type=MESH)

    greet(depth, other)

    @pl.when(place > 0)
    def _():
        greet(depth - 1, half)
        greet(depth - 1, other)

    @pl.when(place < SEG - 1)
    def _():
        greet(depth + 1, half)
        greet(depth + 1, other)

    for one, two in GREETS:
        @pl.when(place == one)
        def _():
            greet(depth + (two - one), half)

        @pl.when(place == two)
        def _():
            greet(depth - (two - one), half)

    at_edge = jnp.logical_or(place == 0, place == SEG - 1)
    callers = jnp.where(at_edge, 3, 5)
    for pair in GREETS:
        callers = callers + jnp.where(any_of(place, pair), 1, 0)

    load_sources.wait()
    load_ahead.wait()

    @pl.when(place == 0)
    def _():
        for row in range(HALF):
            reduced[base + row] = sources[:, row * BLK:(row + 1) * BLK].astype(BF16)

    @pl.when(place > 0)
    def _():
        split_couplings(raw.at[0], diag_ahead, side_ahead, base)
        for row in range(HALF):
            rounded[row] = sources[:, row * BLK:(row + 1) * BLK].astype(BF16)

    pl.semaphore_wait(barrier, callers)

    def tell(table):
        for one, two, slot in table:
            @pl.when(place == one)
            def _():
                pl.semaphore_signal(
                    go.at[slot], inc=1, device_id=(depth + (two - one), half), device_id_type=MESH
                )

    def wait_told(slot, among):
        places = [two for _, two, kind in TOLD if kind == slot and two in among]

        @pl.when(any_of(place, places))
        def _():
            pl.semaphore_wait(go.at[slot], 1)

    def once(source, target, slot, step, lat):
        return pltpu.make_async_remote_copy(
            src_ref=source, dst_ref=target, send_sem=once_send.at[slot], recv_sem=once_recv.at[slot],
            device_id=(depth + step, lat), device_id_type=MESH,
        )

    mine = pl.ds(base, HALF)
    theirs = pl.ds(their_base, HALF)
    swaps_ahead = any_of(place, SWAP_AHEAD)
    swaps_behind = any_of(place, SWAP_BEHIND)
    ahead_swaps = any_of(place + 1, SWAP_AHEAD)
    behind_swaps = any_of(place - 1, SWAP_BEHIND)
    give_reduced = once(reduced.at[mine], reduced.at[mine], 0, 0, other)
    take_reduced = once(reduced.at[theirs], reduced.at[theirs], 0, 0, other)
    give_pulled = once(pulled.at[mine], pulled.at[mine], 7, 0, other)
    take_pulled = once(pulled.at[theirs], pulled.at[theirs], 7, 0, other)
    give_pattern = once(pattern, their_pattern, 1, 0, other)
    give_source = once(rounded, source_next, 2, -1, half)
    give_diag_ahead = once(diag_ahead, diag_next, 3, -1, half)
    give_diag_behind = once(diag_behind, diag_prior, 4, 1, half)

    def side_copy(blocks, kind, owner, first, rows):
        part = blocks.at[pl.ds(owner * HALF + first, rows)]
        return once(part, part, 5 + kind, 0, other)

    def give_side(blocks, kind, paces, places, first=lambda: None):
        for pace in sorted(set(paces[p] for p in places if paces[p])):
            group = [p for p in places if paces[p] == pace]

            @pl.when(any_of(place, group))
            def _():
                wait_told(kind, group)
                first()

                def part(step, carry):
                    copy = side_copy(blocks, kind, half, step * pace, pace)
                    copy.start()
                    copy.wait_send()
                    return carry

                lax.fori_loop(0, HALF // pace, part, 0)

    def take_side(blocks, kind):
        side_copy(blocks, kind, other, 0, HALF).wait_recv()

    def chunk_copy(source, target, chunk, kind, owner, step, send, recv):
        return pltpu.make_async_remote_copy(
            src_ref=source.at[kind // 2, pl.ds(chunk * ROWS, ROWS)],
            dst_ref=target.at[pl.ds(owner * HALF + chunk * ROWS, ROWS)],
            send_sem=send.at[kind, chunk], recv_sem=recv.at[kind, chunk],
            device_id=(depth + step, other if kind else half), device_id_type=MESH,
        )

    def forward_copy(chunk, kind, owner):
        return chunk_copy(out_fwd, incoming_plus if kind == 2 else incoming, chunk, kind, owner, 1, fwd_send, fwd_recv)

    def backward_copy(chunk, kind, owner):
        return chunk_copy(out_bwd, later_plus if kind == 2 else later, chunk, kind, owner, -1, bwd_send, bwd_recv)

    def wait_arrivals(make, kinds):
        for kind in kinds:
            for chunk in range(CHUNKS):
                make(chunk, kind, other if kind else half).wait_recv()

    def wait_sent(make, swaps):
        for kind in (0, 1):
            for chunk in range(CHUNKS):
                make(chunk, kind, half).wait_send()

        @pl.when(jnp.logical_not(swaps))
        def _():
            for chunk in range(CHUNKS):
                make(chunk, 2, half).wait_send()

    def in_chunks(make, out, compute, ahead_of, swaps):
        for chunk in range(CHUNKS + 1):
            if chunk < CHUNKS:
                for row in range(chunk * ROWS, (chunk + 1) * ROWS):
                    out[0, row] = compute(row).astype(BF16)
                make(chunk, 1, half).start()
                make(chunk, 0, half).start()
            if chunk > 0:
                for row in range((chunk - 1) * ROWS, chunk * ROWS):
                    out[1, row] = ahead_of(out[0, row], row).astype(BF16)

                @pl.when(jnp.logical_not(swaps))
                def _():
                    make(chunk - 1, 2, half).start()

    def next_source(sent, row):
        return source_next[row] - dot(sent, diag_next[row])

    def prior_pulled(sent, row):
        return dot(sent, diag_prior[row])

    @pl.when(place == 0)
    def _():
        give_reduced.start()
        give_reduced.wait_send()

    tell(AFTER_START)
    give_pattern.start()

    @pl.when(jnp.logical_and(place > 0, jnp.logical_not(swaps_ahead)))
    def _():
        give_source.start()
        give_diag_ahead.start()

    give_side(side_ahead, AHEAD, PACE_AHEAD, FIRST_AHEAD)

    load_behind.wait()

    def take_diag_prior():
        @pl.when(jnp.logical_not(behind_swaps))
        def _():
            give_diag_behind.wait_recv()

    def prepare_behind():
        split_couplings(raw.at[1], diag_behind, side_behind, base)

    def start_diag_behind():
        @pl.when(jnp.logical_not(swaps_behind))
        def _():
            give_diag_behind.start()

    @pl.when(place < SEG - 1)
    def _():
        prepare_behind()

        @pl.when(lax.rem(place, 2) == 0)
        def _():
            start_diag_behind()

    load_factor.wait()
    transpose_factor(factor)

    give_side(side_ahead, AHEAD, PACE_AHEAD, [p for p in range(1, SEG) if p not in FIRST_AHEAD])
    give_pattern.wait_recv()
    load_cols = pltpu.make_async_copy(their_pattern, their_cols, load_sem.at[3])
    load_cols.start()
    load_cols.wait()

    @pl.when(place == 0)
    def _():
        take_reduced.wait_recv()

    def forward_row(row):
        value = row_apply(factor, reduced, cols, row)
        field[row] = value
        return value

    def last_row(row):
        value = row_apply(factor, reduced, cols, row)
        swept[:, row * BLK:(row + 1) * BLK] = value
        return value

    def backward_row(row):
        value = field[row] - row_apply(factor, pulled, cols, row)
        swept[:, row * BLK:(row + 1) * BLK] = value
        return value

    @pl.when(place > 0)
    def _():
        wait_arrivals(forward_copy, (0,))
        for row in range(HALF):
            near = dot(incoming[base + row], diag_ahead[row])
            partial[row] = sources[:, row * BLK:(row + 1) * BLK] - near
        wait_arrivals(forward_copy, (1,))
        for row in range(HALF):
            beside = dot(incoming[cols[1, row]], side_ahead[base + row])
            reduced[base + row] = (partial[row] - beside).astype(BF16)

        @pl.when(swaps_ahead)
        def _():
            give_reduced.start()
            take_reduced.wait_recv()

        @pl.when(jnp.logical_not(swaps_ahead))
        def _():
            take_side(side_ahead, AHEAD)
            for row in range(HALF):
                theirs_part[row] = dot(incoming[their_cols[1, row]], side_ahead[their_base + row])
            wait_arrivals(forward_copy, (2,))
            for row in range(HALF):
                reduced[their_base + row] = (incoming_plus[their_base + row] - theirs_part[row]).astype(BF16)

    @pl.when(jnp.logical_and(place < SEG - 1, jnp.logical_not(ahead_swaps)))
    def _():
        give_source.wait_recv()
        give_diag_ahead.wait_recv()

    @pl.when(place == SEG - 1)
    def _():
        take_diag_prior()
        in_chunks(backward_copy, out_bwd, last_row, prior_pulled, behind_swaps)

    @pl.when(place < SEG - 1)
    def _():
        in_chunks(forward_copy, out_fwd, forward_row, next_source, ahead_swaps)

    tell(AT_FORWARD)

    @pl.when(place == 3)
    def _():
        start_diag_behind()

    def start_diag_far():
        @pl.when(any_of(place, (1, 5)))
        def _():
            start_diag_behind()


    give_side(side_behind, BEHIND, PACE_BEHIND, range(SEG - 1), start_diag_far)

    @pl.when(place < SEG - 1)
    def _():
        wait_sent(forward_copy, ahead_swaps)

    @pl.when(place < SEG - 1)
    def _():
        wait_arrivals(backward_copy, (0,))
        for row in range(HALF):
            partial[row] = dot(later[base + row], diag_behind[row])
        wait_arrivals(backward_copy, (1,))
        for row in range(HALF):
            beside = dot(later[cols[1, row]], side_behind[base + row])
            pulled[base + row] = (partial[row] + beside).astype(BF16)

        @pl.when(swaps_behind)
        def _():
            give_pulled.start()
            take_pulled.wait_recv()

        @pl.when(jnp.logical_not(swaps_behind))
        def _():
            take_side(side_behind, BEHIND)
            for row in range(HALF):
                theirs_part[row] = dot(later[their_cols[1, row]], side_behind[their_base + row])
            wait_arrivals(backward_copy, (2,))
            for row in range(HALF):
                pulled[their_base + row] = (later_plus[their_base + row] + theirs_part[row]).astype(BF16)

        @pl.when(place > 0)
        def _():
            take_diag_prior()
            in_chunks(backward_copy, out_bwd, backward_row, prior_pulled, behind_swaps)

        @pl.when(place == 0)
        def _():
            for row in range(HALF):
                backward_row(row)


    tell(AT_BACKWARD)

    @pl.when(place > 0)
    def _():
        wait_sent(backward_copy, behind_swaps)

    @pl.when(swaps_ahead)
    def _():
        give_reduced.wait_send()

    @pl.when(swaps_behind)
    def _():
        give_pulled.wait_send()

    give_pattern.wait_send()

    @pl.when(jnp.logical_and(place > 0, jnp.logical_not(swaps_ahead)))
    def _():
        give_source.wait_send()
        give_diag_ahead.wait_send()

    @pl.when(jnp.logical_and(place < SEG - 1, jnp.logical_not(swaps_behind)))
    def _():
        give_diag_behind.wait_send()


def local(sources, frontal, couplings, pattern):
    vector = pltpu.VMEM((NBR, SHOTS, BLK), BF16)
    half_vector = pltpu.VMEM((HALF, SHOTS, BLK), BF16)
    half_double = pltpu.VMEM((2, HALF, SHOTS, BLK), BF16)
    half_blocks = pltpu.VMEM((HALF, BLK, BLK), BF16)
    blocks = pltpu.VMEM((NBR, BLK, BLK), BF16)
    vmem = pl.BlockSpec(memory_space=pltpu.VMEM)
    hbm = pl.BlockSpec(memory_space=pl.ANY)
    smem = pl.BlockSpec(memory_space=pltpu.SMEM)
    chunk_sem = pltpu.SemaphoreType.DMA((3, CHUNKS))
    columns = pattern[0].T
    once_sem = pltpu.SemaphoreType.DMA((8,))
    out = pl.pallas_call(
        sweep_kernel,
        out_shape=jax.ShapeDtypeStruct((SHOTS, HALF * BLK), F32),
        in_specs=[hbm, hbm, hbm, hbm, smem],
        out_specs=vmem,
        scratch_shapes=[
            pltpu.VMEM((SHOTS, HALF * BLK), F32),
            pltpu.VMEM((HALF, SHOTS, BLK), F32),
            pltpu.VMEM((HALF, SHOTS, BLK), F32),
            pltpu.VMEM((HALF, KH, BLK, BLK), BF16),
            pltpu.VMEM((2, HALF, KC, BLK, BLK), BF16),
            half_blocks, half_blocks, blocks, blocks, half_blocks, half_blocks,
            half_vector, half_vector,
            pltpu.VMEM((KH, HALF), jnp.int32),
            pltpu.SMEM((KH, HALF), jnp.int32),
            pltpu.VMEM((HALF, SHOTS, BLK), F32),
            vector, vector, vector, vector, vector, vector, half_double, half_double,
            pltpu.SemaphoreType.DMA((5,)),
            once_sem, once_sem, chunk_sem, chunk_sem, chunk_sem, chunk_sem,
            pltpu.SemaphoreType.REGULAR((2,)),
        ],
        compiler_params=pltpu.CompilerParams(
            collective_id=0, has_side_effects=True, vmem_limit_bytes=60 * 1024 * 1024
        ),
    )(sources[0], frontal[0], couplings[0], columns, columns)
    return out[None]


def solution(mesh):
    return jax.shard_map(
        local,
        mesh=mesh,
        in_specs=(
            P("depth", None, "lat"),
            P("depth", "lat", None, None, None),
            P("depth", None, "lat", None, None, None),
            P("depth", "lat", None),
        ),
        out_specs=P("depth", None, "lat"),
        check_vma=False,
    )
```

```python
import jax
import jax.numpy as jnp
from jax import lax
from jax.experimental import pallas as pl
from jax.experimental.pallas import tpu as pltpu
from jax.sharding import PartitionSpec as P

MESH = pl.DeviceIdType.MESH
BLK = 128
KH = 8
KC = 2
SEG = 8
SHOTS = 16
NBR = 48
HALF = 24
CHUNKS = 3
ROWS = HALF // CHUNKS
F32 = jnp.float32
BF16 = jnp.bfloat16
NN = (((1,), (0,)), ((), ()))

SWAP_AHEAD = (2,)
SWAP_BEHIND = (6,)
AHEAD, BEHIND = range(2)
AFTER_START = ()
AT_FORWARD = ((0, 4, AHEAD), (1, 5, AHEAD), (3, 7, AHEAD))
AT_BACKWARD = ((6, 2, BEHIND), (6, 3, BEHIND), (4, 1, BEHIND))
PACE_AHEAD = (0, 24, 0, 24, 4, 3, 12, 8)
PACE_BEHIND = (4, 24, 4, 8, 3, 4, 0, 0)
FIRST_AHEAD = (1, 3, 6)
PACES = (PACE_AHEAD, PACE_BEHIND)
AFTER_START = tuple(told for told in AFTER_START if PACES[told[2]][told[1]])
AT_FORWARD = tuple(told for told in AT_FORWARD if PACES[told[2]][told[1]])
AT_BACKWARD = tuple(told for told in AT_BACKWARD if PACES[told[2]][told[1]])
TOLD = AFTER_START + AT_FORWARD + AT_BACKWARD
GREETS = tuple(sorted({(min(i, j), max(i, j)) for i, j, _ in TOLD if abs(i - j) > 1}))


def any_of(place, places):
    found = place < 0
    for one in places:
        found = jnp.logical_or(found, place == one)
    return found


def dot(operand, weights):
    return lax.dot_general(operand, weights, NN, preferred_element_type=F32)


def gathered(vector, cols, row, count):
    return jnp.concatenate([vector[cols[k, row]] for k in range(count)], axis=1)


def row_apply(blocks, vector, cols, row):
    return dot(gathered(vector, cols, row, KH), blocks[row].reshape(KH * BLK, BLK))


def transpose_factor(blocks):
    def one(row, carry):
        for k in range(KH):
            blocks[row, k] = blocks[row, k].T
        return carry

    lax.fori_loop(0, HALF, one, 0, unroll=2)


def split_couplings(raw, diagonal, beside, base):
    def one(row, carry):
        diagonal[row] = raw[row, 0].T
        beside[base + row] = raw[row, 1].T
        return carry

    lax.fori_loop(0, HALF, one, 0, unroll=4)


def sweep_kernel(
    sources_hbm, frontal, couplings, pattern, cols, swept,
    sources, partial, theirs_part, factor, raw, diag_ahead, diag_behind, side_ahead, side_behind, diag_next, diag_prior,
    rounded, source_next, their_pattern, their_cols, field, incoming, later, incoming_plus, later_plus, reduced, pulled, out_fwd, out_bwd,
    load_sem, once_send, once_recv, fwd_send, fwd_recv, bwd_send, bwd_recv, go,
):
    depth = lax.axis_index("depth")
    half = lax.axis_index("lat")
    place = lax.rem(depth, SEG)
    other = 1 - half
    base = half * HALF
    their_base = other * HALF

    load_factor = pltpu.make_async_copy(frontal, factor, load_sem.at[0])
    load_ahead = pltpu.make_async_copy(couplings.at[0], raw.at[0], load_sem.at[1])
    load_behind = pltpu.make_async_copy(couplings.at[1], raw.at[1], load_sem.at[2])
    load_sources = pltpu.make_async_copy(sources_hbm, sources, load_sem.at[4])
    load_sources.start()
    load_ahead.start()
    load_factor.start()
    load_behind.start()

    barrier = pltpu.get_barrier_semaphore()

    def greet(depth_index, lat):
        pl.semaphore_signal(barrier, inc=1, device_id=(depth_index, lat), device_id_type=MESH)

    greet(depth, other)

    @pl.when(place > 0)
    def _():
        greet(depth - 1, half)
        greet(depth - 1, other)

    @pl.when(place < SEG - 1)
    def _():
        greet(depth + 1, half)
        greet(depth + 1, other)

    for one, two in GREETS:
        @pl.when(place == one)
        def _():
            greet(depth + (two - one), half)

        @pl.when(place == two)
        def _():
            greet(depth - (two - one), half)

    at_edge = jnp.logical_or(place == 0, place == SEG - 1)
    callers = jnp.where(at_edge, 3, 5)
    for pair in GREETS:
        callers = callers + jnp.where(any_of(place, pair), 1, 0)

    load_sources.wait()
    load_ahead.wait()

    @pl.when(place == 0)
    def _():
        for row in range(HALF):
            reduced[base + row] = sources[:, row * BLK:(row + 1) * BLK].astype(BF16)

    @pl.when(place > 0)
    def _():
        split_couplings(raw.at[0], diag_ahead, side_ahead, base)
        for row in range(HALF):
            rounded[row] = sources[:, row * BLK:(row + 1) * BLK].astype(BF16)

    pl.semaphore_wait(barrier, callers)

    def tell(table):
        for one, two, slot in table:
            @pl.when(place == one)
            def _():
                pl.semaphore_signal(
                    go.at[slot], inc=1, device_id=(depth + (two - one), half), device_id_type=MESH
                )

    def wait_told(slot, among):
        places = [two for _, two, kind in TOLD if kind == slot and two in among]

        @pl.when(any_of(place, places))
        def _():
            pl.semaphore_wait(go.at[slot], 1)

    def once(source, target, slot, step, lat):
        return pltpu.make_async_remote_copy(
            src_ref=source, dst_ref=target, send_sem=once_send.at[slot], recv_sem=once_recv.at[slot],
            device_id=(depth + step, lat), device_id_type=MESH,
        )

    mine = pl.ds(base, HALF)
    theirs = pl.ds(their_base, HALF)
    swaps_ahead = any_of(place, SWAP_AHEAD)
    swaps_behind = any_of(place, SWAP_BEHIND)
    ahead_swaps = any_of(place + 1, SWAP_AHEAD)
    behind_swaps = any_of(place - 1, SWAP_BEHIND)
    give_reduced = once(reduced.at[mine], reduced.at[mine], 0, 0, other)
    take_reduced = once(reduced.at[theirs], reduced.at[theirs], 0, 0, other)
    give_pulled = once(pulled.at[mine], pulled.at[mine], 7, 0, other)
    take_pulled = once(pulled.at[theirs], pulled.at[theirs], 7, 0, other)
    give_pattern = once(pattern, their_pattern, 1, 0, other)
    give_source = once(rounded, source_next, 2, -1, half)
    give_diag_ahead = once(diag_ahead, diag_next, 3, -1, half)
    give_diag_behind = once(diag_behind, diag_prior, 4, 1, half)

    def side_copy(blocks, kind, owner, first, rows):
        part = blocks.at[pl.ds(owner * HALF + first, rows)]
        return once(part, part, 5 + kind, 0, other)

    def give_side(blocks, kind, paces, places):
        for pace in sorted(set(paces[p] for p in places if paces[p])):
            group = [p for p in places if paces[p] == pace]

            @pl.when(any_of(place, group))
            def _():
                wait_told(kind, group)

                def part(step, carry):
                    copy = side_copy(blocks, kind, half, step * pace, pace)
                    copy.start()
                    copy.wait_send()
                    return carry

                lax.fori_loop(0, HALF // pace, part, 0)

    def take_side(blocks, kind):
        side_copy(blocks, kind, other, 0, HALF).wait_recv()

    def chunk_copy(source, target, chunk, kind, owner, step, send, recv):
        return pltpu.make_async_remote_copy(
            src_ref=source.at[kind // 2, pl.ds(chunk * ROWS, ROWS)],
            dst_ref=target.at[pl.ds(owner * HALF + chunk * ROWS, ROWS)],
            send_sem=send.at[kind, chunk], recv_sem=recv.at[kind, chunk],
            device_id=(depth + step, other if kind else half), device_id_type=MESH,
        )

    def forward_copy(chunk, kind, owner):
        return chunk_copy(out_fwd, incoming_plus if kind == 2 else incoming, chunk, kind, owner, 1, fwd_send, fwd_recv)

    def backward_copy(chunk, kind, owner):
        return chunk_copy(out_bwd, later_plus if kind == 2 else later, chunk, kind, owner, -1, bwd_send, bwd_recv)

    def wait_arrivals(make, kinds):
        for kind in kinds:
            for chunk in range(CHUNKS):
                make(chunk, kind, other if kind else half).wait_recv()

    def wait_sent(make, swaps):
        for kind in (0, 1):
            for chunk in range(CHUNKS):
                make(chunk, kind, half).wait_send()

        @pl.when(jnp.logical_not(swaps))
        def _():
            for chunk in range(CHUNKS):
                make(chunk, 2, half).wait_send()

    def in_chunks(make, out, compute, ahead_of, swaps):
        for chunk in range(CHUNKS + 1):
            if chunk < CHUNKS:
                for row in range(chunk * ROWS, (chunk + 1) * ROWS):
                    out[0, row] = compute(row).astype(BF16)
                make(chunk, 1, half).start()
                make(chunk, 0, half).start()
            if chunk > 0:
                for row in range((chunk - 1) * ROWS, chunk * ROWS):
                    out[1, row] = ahead_of(out[0, row], row).astype(BF16)

                @pl.when(jnp.logical_not(swaps))
                def _():
                    make(chunk - 1, 2, half).start()

    def next_source(sent, row):
        return source_next[row] - dot(sent, diag_next[row])

    def prior_pulled(sent, row):
        return dot(sent, diag_prior[row])

    @pl.when(place == 0)
    def _():
        give_reduced.start()
        give_reduced.wait_send()

    tell(AFTER_START)
    give_pattern.start()

    @pl.when(jnp.logical_and(place > 0, jnp.logical_not(swaps_ahead)))
    def _():
        give_source.start()
        give_diag_ahead.start()

    give_side(side_ahead, AHEAD, PACE_AHEAD, FIRST_AHEAD)

    load_behind.wait()

    def take_diag_prior():
        @pl.when(jnp.logical_not(behind_swaps))
        def _():
            give_diag_behind.wait_recv()

    def prepare_behind():
        split_couplings(raw.at[1], diag_behind, side_behind, base)

    def start_diag_behind():
        @pl.when(jnp.logical_not(swaps_behind))
        def _():
            give_diag_behind.start()

    @pl.when(place < SEG - 1)
    def _():
        prepare_behind()

        @pl.when(lax.rem(place, 2) == 0)
        def _():
            start_diag_behind()

    load_factor.wait()
    transpose_factor(factor)

    give_side(side_ahead, AHEAD, PACE_AHEAD, [p for p in range(1, SEG) if p not in FIRST_AHEAD])
    give_pattern.wait_recv()
    load_cols = pltpu.make_async_copy(their_pattern, their_cols, load_sem.at[3])
    load_cols.start()
    load_cols.wait()

    @pl.when(place == 0)
    def _():
        take_reduced.wait_recv()

    def forward_row(row):
        value = row_apply(factor, reduced, cols, row)
        field[row] = value
        return value

    def last_row(row):
        value = row_apply(factor, reduced, cols, row)
        swept[:, row * BLK:(row + 1) * BLK] = value
        return value

    def backward_row(row):
        value = field[row] - row_apply(factor, pulled, cols, row)
        swept[:, row * BLK:(row + 1) * BLK] = value
        return value

    @pl.when(place > 0)
    def _():
        wait_arrivals(forward_copy, (0,))
        for row in range(HALF):
            near = dot(incoming[base + row], diag_ahead[row])
            partial[row] = sources[:, row * BLK:(row + 1) * BLK] - near
        wait_arrivals(forward_copy, (1,))
        for row in range(HALF):
            beside = dot(incoming[cols[1, row]], side_ahead[base + row])
            reduced[base + row] = (partial[row] - beside).astype(BF16)

        @pl.when(swaps_ahead)
        def _():
            give_reduced.start()
            take_reduced.wait_recv()

        @pl.when(jnp.logical_not(swaps_ahead))
        def _():
            take_side(side_ahead, AHEAD)
            for row in range(HALF):
                theirs_part[row] = dot(incoming[their_cols[1, row]], side_ahead[their_base + row])
            wait_arrivals(forward_copy, (2,))
            for row in range(HALF):
                reduced[their_base + row] = (incoming_plus[their_base + row] - theirs_part[row]).astype(BF16)

    @pl.when(jnp.logical_and(place < SEG - 1, jnp.logical_not(ahead_swaps)))
    def _():
        give_source.wait_recv()
        give_diag_ahead.wait_recv()

    @pl.when(place == SEG - 1)
    def _():
        take_diag_prior()
        in_chunks(backward_copy, out_bwd, last_row, prior_pulled, behind_swaps)

    @pl.when(place < SEG - 1)
    def _():
        in_chunks(forward_copy, out_fwd, forward_row, next_source, ahead_swaps)

    tell(AT_FORWARD)

    @pl.when(place < SEG - 1)
    def _():
        wait_sent(forward_copy, ahead_swaps)

        @pl.when(lax.rem(place, 2) == 1)
        def _():
            start_diag_behind()

    give_side(side_behind, BEHIND, PACE_BEHIND, range(SEG - 1))

    @pl.when(place < SEG - 1)
    def _():
        wait_arrivals(backward_copy, (0,))
        for row in range(HALF):
            partial[row] = dot(later[base + row], diag_behind[row])
        wait_arrivals(backward_copy, (1,))
        for row in range(HALF):
            beside = dot(later[cols[1, row]], side_behind[base + row])
            pulled[base + row] = (partial[row] + beside).astype(BF16)

        @pl.when(swaps_behind)
        def _():
            give_pulled.start()
            take_pulled.wait_recv()

        @pl.when(jnp.logical_not(swaps_behind))
        def _():
            take_side(side_behind, BEHIND)
            for row in range(HALF):
                theirs_part[row] = dot(later[their_cols[1, row]], side_behind[their_base + row])
            wait_arrivals(backward_copy, (2,))
            for row in range(HALF):
                pulled[their_base + row] = (later_plus[their_base + row] + theirs_part[row]).astype(BF16)

        @pl.when(place > 0)
        def _():
            take_diag_prior()
            in_chunks(backward_copy, out_bwd, backward_row, prior_pulled, behind_swaps)

        @pl.when(place == 0)
        def _():
            for row in range(HALF):
                backward_row(row)


    tell(AT_BACKWARD)

    @pl.when(place > 0)
    def _():
        wait_sent(backward_copy, behind_swaps)

    @pl.when(swaps_ahead)
    def _():
        give_reduced.wait_send()

    @pl.when(swaps_behind)
    def _():
        give_pulled.wait_send()

    give_pattern.wait_send()

    @pl.when(jnp.logical_and(place > 0, jnp.logical_not(swaps_ahead)))
    def _():
        give_source.wait_send()
        give_diag_ahead.wait_send()

    @pl.when(jnp.logical_and(place < SEG - 1, jnp.logical_not(swaps_behind)))
    def _():
        give_diag_behind.wait_send()


def local(sources, frontal, couplings, pattern):
    vector = pltpu.VMEM((NBR, SHOTS, BLK), BF16)
    half_vector = pltpu.VMEM((HALF, SHOTS, BLK), BF16)
    half_double = pltpu.VMEM((2, HALF, SHOTS, BLK), BF16)
    half_blocks = pltpu.VMEM((HALF, BLK, BLK), BF16)
    blocks = pltpu.VMEM((NBR, BLK, BLK), BF16)
    vmem = pl.BlockSpec(memory_space=pltpu.VMEM)
    hbm = pl.BlockSpec(memory_space=pl.ANY)
    smem = pl.BlockSpec(memory_space=pltpu.SMEM)
    chunk_sem = pltpu.SemaphoreType.DMA((3, CHUNKS))
    columns = pattern[0].T
    once_sem = pltpu.SemaphoreType.DMA((8,))
    out = pl.pallas_call(
        sweep_kernel,
        out_shape=jax.ShapeDtypeStruct((SHOTS, HALF * BLK), F32),
        in_specs=[hbm, hbm, hbm, hbm, smem],
        out_specs=vmem,
        scratch_shapes=[
            pltpu.VMEM((SHOTS, HALF * BLK), F32),
            pltpu.VMEM((HALF, SHOTS, BLK), F32),
            pltpu.VMEM((HALF, SHOTS, BLK), F32),
            pltpu.VMEM((HALF, KH, BLK, BLK), BF16),
            pltpu.VMEM((2, HALF, KC, BLK, BLK), BF16),
            half_blocks, half_blocks, blocks, blocks, half_blocks, half_blocks,
            half_vector, half_vector,
            pltpu.VMEM((KH, HALF), jnp.int32),
            pltpu.SMEM((KH, HALF), jnp.int32),
            pltpu.VMEM((HALF, SHOTS, BLK), F32),
            vector, vector, vector, vector, vector, vector, half_double, half_double,
            pltpu.SemaphoreType.DMA((5,)),
            once_sem, once_sem, chunk_sem, chunk_sem, chunk_sem, chunk_sem,
            pltpu.SemaphoreType.REGULAR((2,)),
        ],
        compiler_params=pltpu.CompilerParams(
            collective_id=0, has_side_effects=True, vmem_limit_bytes=60 * 1024 * 1024
        ),
    )(sources[0], frontal[0], couplings[0], columns, columns)
    return out[None]


def solution(mesh):
    return jax.shard_map(
        local,
        mesh=mesh,
        in_specs=(
            P("depth", None, "lat"),
            P("depth", "lat", None, None, None),
            P("depth", None, "lat", None, None, None),
            P("depth", "lat", None),
        ),
        out_specs=P("depth", None, "lat"),
        check_vma=False,
    )
```

```python
import jax
import jax.numpy as jnp
from jax import lax
from jax.experimental import pallas as pl
from jax.experimental.pallas import tpu as pltpu
from jax.sharding import PartitionSpec as P

MESH = pl.DeviceIdType.MESH
BLK = 128
KH = 8
KC = 2
SEG = 8
SHOTS = 16
NBR = 48
HALF = 24
CHUNKS = 3
ROWS = HALF // CHUNKS
F32 = jnp.float32
BF16 = jnp.bfloat16
NN = (((1,), (0,)), ((), ()))

SWAP_AHEAD = (2,)
SWAP_BEHIND = (6,)
AHEAD, BEHIND = range(2)
AFTER_START = ()
AT_FORWARD = ((0, 4, AHEAD), (1, 5, AHEAD), (3, 7, AHEAD))
AT_BACKWARD = ((6, 3, BEHIND), (5, 2, BEHIND), (4, 1, BEHIND))
PACE_AHEAD = (0, 24, 0, 24, 4, 3, 12, 8)
PACE_BEHIND = (4, 24, 8, 8, 3, 4, 0, 0)
FIRST_AHEAD = (1, 3, 6)
PACES = (PACE_AHEAD, PACE_BEHIND)
AFTER_START = tuple(told for told in AFTER_START if PACES[told[2]][told[1]])
AT_FORWARD = tuple(told for told in AT_FORWARD if PACES[told[2]][told[1]])
AT_BACKWARD = tuple(told for told in AT_BACKWARD if PACES[told[2]][told[1]])
TOLD = AFTER_START + AT_FORWARD + AT_BACKWARD
GREETS = tuple(sorted({(min(i, j), max(i, j)) for i, j, _ in TOLD if abs(i - j) > 1}))


def any_of(place, places):
    found = place < 0
    for one in places:
        found = jnp.logical_or(found, place == one)
    return found


def dot(operand, weights):
    return lax.dot_general(operand, weights, NN, preferred_element_type=F32)


def gathered(vector, cols, row, count):
    return jnp.concatenate([vector[cols[k, row]] for k in range(count)], axis=1)


def row_apply(blocks, vector, cols, row):
    return dot(gathered(vector, cols, row, KH), blocks[row].reshape(KH * BLK, BLK))


def transpose_factor(blocks):
    def one(row, carry):
        for k in range(KH):
            blocks[row, k] = blocks[row, k].T
        return carry

    lax.fori_loop(0, HALF, one, 0, unroll=2)


def split_couplings(raw, diagonal, beside, base):
    def one(row, carry):
        diagonal[row] = raw[row, 0].T
        beside[base + row] = raw[row, 1].T
        return carry

    lax.fori_loop(0, HALF, one, 0, unroll=4)


def sweep_kernel(
    sources_hbm, frontal, couplings, pattern, cols, swept,
    sources, partial, theirs_part, factor, raw, diag_ahead, diag_behind, side_ahead, side_behind, diag_next, diag_prior,
    rounded, source_next, their_pattern, their_cols, field, incoming, later, incoming_plus, later_plus, reduced, pulled, out_fwd, out_bwd,
    load_sem, once_send, once_recv, fwd_send, fwd_recv, bwd_send, bwd_recv, go,
):
    depth = lax.axis_index("depth")
    half = lax.axis_index("lat")
    place = lax.rem(depth, SEG)
    other = 1 - half
    base = half * HALF
    their_base = other * HALF

    load_factor = pltpu.make_async_copy(frontal, factor, load_sem.at[0])
    load_ahead = pltpu.make_async_copy(couplings.at[0], raw.at[0], load_sem.at[1])
    load_behind = pltpu.make_async_copy(couplings.at[1], raw.at[1], load_sem.at[2])
    load_sources = pltpu.make_async_copy(sources_hbm, sources, load_sem.at[4])
    load_sources.start()
    load_ahead.start()
    load_factor.start()
    load_behind.start()

    barrier = pltpu.get_barrier_semaphore()

    def greet(depth_index, lat):
        pl.semaphore_signal(barrier, inc=1, device_id=(depth_index, lat), device_id_type=MESH)

    greet(depth, other)

    @pl.when(place > 0)
    def _():
        greet(depth - 1, half)
        greet(depth - 1, other)

    @pl.when(place < SEG - 1)
    def _():
        greet(depth + 1, half)
        greet(depth + 1, other)

    for one, two in GREETS:
        @pl.when(place == one)
        def _():
            greet(depth + (two - one), half)

        @pl.when(place == two)
        def _():
            greet(depth - (two - one), half)

    at_edge = jnp.logical_or(place == 0, place == SEG - 1)
    callers = jnp.where(at_edge, 3, 5)
    for pair in GREETS:
        callers = callers + jnp.where(any_of(place, pair), 1, 0)

    load_sources.wait()
    load_ahead.wait()

    @pl.when(place == 0)
    def _():
        for row in range(HALF):
            reduced[base + row] = sources[:, row * BLK:(row + 1) * BLK].astype(BF16)

    @pl.when(place > 0)
    def _():
        split_couplings(raw.at[0], diag_ahead, side_ahead, base)
        for row in range(HALF):
            rounded[row] = sources[:, row * BLK:(row + 1) * BLK].astype(BF16)

    pl.semaphore_wait(barrier, callers)

    def tell(table):
        for one, two, slot in table:
            @pl.when(place == one)
            def _():
                pl.semaphore_signal(
                    go.at[slot], inc=1, device_id=(depth + (two - one), half), device_id_type=MESH
                )

    def wait_told(slot, among):
        places = [two for _, two, kind in TOLD if kind == slot and two in among]

        @pl.when(any_of(place, places))
        def _():
            pl.semaphore_wait(go.at[slot], 1)

    def once(source, target, slot, step, lat):
        return pltpu.make_async_remote_copy(
            src_ref=source, dst_ref=target, send_sem=once_send.at[slot], recv_sem=once_recv.at[slot],
            device_id=(depth + step, lat), device_id_type=MESH,
        )

    mine = pl.ds(base, HALF)
    theirs = pl.ds(their_base, HALF)
    swaps_ahead = any_of(place, SWAP_AHEAD)
    swaps_behind = any_of(place, SWAP_BEHIND)
    ahead_swaps = any_of(place + 1, SWAP_AHEAD)
    behind_swaps = any_of(place - 1, SWAP_BEHIND)
    give_reduced = once(reduced.at[mine], reduced.at[mine], 0, 0, other)
    take_reduced = once(reduced.at[theirs], reduced.at[theirs], 0, 0, other)
    give_pulled = once(pulled.at[mine], pulled.at[mine], 7, 0, other)
    take_pulled = once(pulled.at[theirs], pulled.at[theirs], 7, 0, other)
    give_pattern = once(pattern, their_pattern, 1, 0, other)
    give_source = once(rounded, source_next, 2, -1, half)
    give_diag_ahead = once(diag_ahead, diag_next, 3, -1, half)
    give_diag_behind = once(diag_behind, diag_prior, 4, 1, half)

    def side_copy(blocks, kind, owner, first, rows):
        part = blocks.at[pl.ds(owner * HALF + first, rows)]
        return once(part, part, 5 + kind, 0, other)

    def give_side(blocks, kind, paces, places):
        for pace in sorted(set(paces[p] for p in places if paces[p])):
            group = [p for p in places if paces[p] == pace]

            @pl.when(any_of(place, group))
            def _():
                wait_told(kind, group)

                def part(step, carry):
                    copy = side_copy(blocks, kind, half, step * pace, pace)
                    copy.start()
                    copy.wait_send()
                    return carry

                lax.fori_loop(0, HALF // pace, part, 0)

    def take_side(blocks, kind):
        side_copy(blocks, kind, other, 0, HALF).wait_recv()

    def chunk_copy(source, target, chunk, kind, owner, step, send, recv):
        return pltpu.make_async_remote_copy(
            src_ref=source.at[kind // 2, pl.ds(chunk * ROWS, ROWS)],
            dst_ref=target.at[pl.ds(owner * HALF + chunk * ROWS, ROWS)],
            send_sem=send.at[kind, chunk], recv_sem=recv.at[kind, chunk],
            device_id=(depth + step, other if kind else half), device_id_type=MESH,
        )

    def forward_copy(chunk, kind, owner):
        return chunk_copy(out_fwd, incoming_plus if kind == 2 else incoming, chunk, kind, owner, 1, fwd_send, fwd_recv)

    def backward_copy(chunk, kind, owner):
        return chunk_copy(out_bwd, later_plus if kind == 2 else later, chunk, kind, owner, -1, bwd_send, bwd_recv)

    def wait_arrivals(make, kinds):
        for kind in kinds:
            for chunk in range(CHUNKS):
                make(chunk, kind, other if kind else half).wait_recv()

    def wait_sent(make, swaps):
        for kind in (0, 1):
            for chunk in range(CHUNKS):
                make(chunk, kind, half).wait_send()

        @pl.when(jnp.logical_not(swaps))
        def _():
            for chunk in range(CHUNKS):
                make(chunk, 2, half).wait_send()

    def in_chunks(make, out, compute, ahead_of, swaps):
        for chunk in range(CHUNKS + 1):
            if chunk < CHUNKS:
                for row in range(chunk * ROWS, (chunk + 1) * ROWS):
                    out[0, row] = compute(row).astype(BF16)
                make(chunk, 1, half).start()
                make(chunk, 0, half).start()
            if chunk > 0:
                for row in range((chunk - 1) * ROWS, chunk * ROWS):
                    out[1, row] = ahead_of(out[0, row], row).astype(BF16)

                @pl.when(jnp.logical_not(swaps))
                def _():
                    make(chunk - 1, 2, half).start()

    def next_source(sent, row):
        return source_next[row] - dot(sent, diag_next[row])

    def prior_pulled(sent, row):
        return dot(sent, diag_prior[row])

    @pl.when(place == 0)
    def _():
        give_reduced.start()
        give_reduced.wait_send()

    tell(AFTER_START)
    give_pattern.start()

    @pl.when(jnp.logical_and(place > 0, jnp.logical_not(swaps_ahead)))
    def _():
        give_source.start()
        give_diag_ahead.start()

    give_side(side_ahead, AHEAD, PACE_AHEAD, FIRST_AHEAD)

    load_behind.wait()

    def take_diag_prior():
        @pl.when(jnp.logical_not(behind_swaps))
        def _():
            give_diag_behind.wait_recv()

    def prepare_behind():
        split_couplings(raw.at[1], diag_behind, side_behind, base)

    def start_diag_behind():
        @pl.when(jnp.logical_not(swaps_behind))
        def _():
            give_diag_behind.start()

    @pl.when(place < SEG - 1)
    def _():
        prepare_behind()

        @pl.when(lax.rem(place, 2) == 0)
        def _():
            start_diag_behind()

    load_factor.wait()
    transpose_factor(factor)

    give_side(side_ahead, AHEAD, PACE_AHEAD, [p for p in range(1, SEG) if p not in FIRST_AHEAD])
    give_pattern.wait_recv()
    load_cols = pltpu.make_async_copy(their_pattern, their_cols, load_sem.at[3])
    load_cols.start()
    load_cols.wait()

    @pl.when(place == 0)
    def _():
        take_reduced.wait_recv()

    def forward_row(row):
        value = row_apply(factor, reduced, cols, row)
        field[row] = value
        return value

    def last_row(row):
        value = row_apply(factor, reduced, cols, row)
        swept[:, row * BLK:(row + 1) * BLK] = value
        return value

    def backward_row(row):
        value = field[row] - row_apply(factor, pulled, cols, row)
        swept[:, row * BLK:(row + 1) * BLK] = value
        return value

    @pl.when(place > 0)
    def _():
        wait_arrivals(forward_copy, (0,))
        for row in range(HALF):
            near = dot(incoming[base + row], diag_ahead[row])
            partial[row] = sources[:, row * BLK:(row + 1) * BLK] - near
        wait_arrivals(forward_copy, (1,))
        for row in range(HALF):
            beside = dot(incoming[cols[1, row]], side_ahead[base + row])
            reduced[base + row] = (partial[row] - beside).astype(BF16)

        @pl.when(swaps_ahead)
        def _():
            give_reduced.start()
            take_reduced.wait_recv()

        @pl.when(jnp.logical_not(swaps_ahead))
        def _():
            take_side(side_ahead, AHEAD)
            for row in range(HALF):
                theirs_part[row] = dot(incoming[their_cols[1, row]], side_ahead[their_base + row])
            wait_arrivals(forward_copy, (2,))
            for row in range(HALF):
                reduced[their_base + row] = (incoming_plus[their_base + row] - theirs_part[row]).astype(BF16)

    @pl.when(jnp.logical_and(place < SEG - 1, jnp.logical_not(ahead_swaps)))
    def _():
        give_source.wait_recv()
        give_diag_ahead.wait_recv()

    @pl.when(place == SEG - 1)
    def _():
        take_diag_prior()
        in_chunks(backward_copy, out_bwd, last_row, prior_pulled, behind_swaps)

    @pl.when(place < SEG - 1)
    def _():
        in_chunks(forward_copy, out_fwd, forward_row, next_source, ahead_swaps)

    tell(AT_FORWARD)

    @pl.when(place < SEG - 1)
    def _():
        wait_sent(forward_copy, ahead_swaps)

        @pl.when(lax.rem(place, 2) == 1)
        def _():
            start_diag_behind()

    give_side(side_behind, BEHIND, PACE_BEHIND, range(SEG - 1))

    @pl.when(place < SEG - 1)
    def _():
        wait_arrivals(backward_copy, (0,))
        for row in range(HALF):
            partial[row] = dot(later[base + row], diag_behind[row])
        wait_arrivals(backward_copy, (1,))
        for row in range(HALF):
            beside = dot(later[cols[1, row]], side_behind[base + row])
            pulled[base + row] = (partial[row] + beside).astype(BF16)

        @pl.when(swaps_behind)
        def _():
            give_pulled.start()
            take_pulled.wait_recv()

        @pl.when(jnp.logical_not(swaps_behind))
        def _():
            take_side(side_behind, BEHIND)
            for row in range(HALF):
                theirs_part[row] = dot(later[their_cols[1, row]], side_behind[their_base + row])
            wait_arrivals(backward_copy, (2,))
            for row in range(HALF):
                pulled[their_base + row] = (later_plus[their_base + row] + theirs_part[row]).astype(BF16)

        @pl.when(place > 0)
        def _():
            take_diag_prior()
            in_chunks(backward_copy, out_bwd, backward_row, prior_pulled, behind_swaps)

        @pl.when(place == 0)
        def _():
            for row in range(HALF):
                backward_row(row)


    tell(AT_BACKWARD)

    @pl.when(place > 0)
    def _():
        wait_sent(backward_copy, behind_swaps)

    @pl.when(swaps_ahead)
    def _():
        give_reduced.wait_send()

    @pl.when(swaps_behind)
    def _():
        give_pulled.wait_send()

    give_pattern.wait_send()

    @pl.when(jnp.logical_and(place > 0, jnp.logical_not(swaps_ahead)))
    def _():
        give_source.wait_send()
        give_diag_ahead.wait_send()

    @pl.when(jnp.logical_and(place < SEG - 1, jnp.logical_not(swaps_behind)))
    def _():
        give_diag_behind.wait_send()


def local(sources, frontal, couplings, pattern):
    vector = pltpu.VMEM((NBR, SHOTS, BLK), BF16)
    half_vector = pltpu.VMEM((HALF, SHOTS, BLK), BF16)
    half_double = pltpu.VMEM((2, HALF, SHOTS, BLK), BF16)
    half_blocks = pltpu.VMEM((HALF, BLK, BLK), BF16)
    blocks = pltpu.VMEM((NBR, BLK, BLK), BF16)
    vmem = pl.BlockSpec(memory_space=pltpu.VMEM)
    hbm = pl.BlockSpec(memory_space=pl.ANY)
    smem = pl.BlockSpec(memory_space=pltpu.SMEM)
    chunk_sem = pltpu.SemaphoreType.DMA((3, CHUNKS))
    columns = pattern[0].T
    once_sem = pltpu.SemaphoreType.DMA((8,))
    out = pl.pallas_call(
        sweep_kernel,
        out_shape=jax.ShapeDtypeStruct((SHOTS, HALF * BLK), F32),
        in_specs=[hbm, hbm, hbm, hbm, smem],
        out_specs=vmem,
        scratch_shapes=[
            pltpu.VMEM((SHOTS, HALF * BLK), F32),
            pltpu.VMEM((HALF, SHOTS, BLK), F32),
            pltpu.VMEM((HALF, SHOTS, BLK), F32),
            pltpu.VMEM((HALF, KH, BLK, BLK), BF16),
            pltpu.VMEM((2, HALF, KC, BLK, BLK), BF16),
            half_blocks, half_blocks, blocks, blocks, half_blocks, half_blocks,
            half_vector, half_vector,
            pltpu.VMEM((KH, HALF), jnp.int32),
            pltpu.SMEM((KH, HALF), jnp.int32),
            pltpu.VMEM((HALF, SHOTS, BLK), F32),
            vector, vector, vector, vector, vector, vector, half_double, half_double,
            pltpu.SemaphoreType.DMA((5,)),
            once_sem, once_sem, chunk_sem, chunk_sem, chunk_sem, chunk_sem,
            pltpu.SemaphoreType.REGULAR((2,)),
        ],
        compiler_params=pltpu.CompilerParams(
            collective_id=0, has_side_effects=True, vmem_limit_bytes=60 * 1024 * 1024
        ),
    )(sources[0], frontal[0], couplings[0], columns, columns)
    return out[None]


def solution(mesh):
    return jax.shard_map(
        local,
        mesh=mesh,
        in_specs=(
            P("depth", None, "lat"),
            P("depth", "lat", None, None, None),
            P("depth", None, "lat", None, None, None),
            P("depth", "lat", None),
        ),
        out_specs=P("depth", None, "lat"),
        check_vma=False,
    )
```

```python
import jax
import jax.numpy as jnp
from jax import lax
from jax.experimental import pallas as pl
from jax.experimental.pallas import tpu as pltpu
from jax.sharding import PartitionSpec as P

MESH = pl.DeviceIdType.MESH
BLK = 128
KH = 8
KC = 2
SEG = 8
SHOTS = 16
NBR = 48
HALF = 24
CHUNKS = 3
ROWS = HALF // CHUNKS
F32 = jnp.float32
BF16 = jnp.bfloat16
NN = (((1,), (0,)), ((), ()))

SWAP_AHEAD = (2,)
SWAP_BEHIND = (6,)
AHEAD, BEHIND = range(2)
AFTER_START = ()
AT_FORWARD = ((0, 4, AHEAD), (1, 5, AHEAD), (3, 7, AHEAD))
AT_BACKWARD = ((6, 3, BEHIND), (5, 2, BEHIND), (4, 1, BEHIND))
PACE_AHEAD = (0, 24, 0, 24, 4, 3, 12, 6)
PACE_BEHIND = (4, 24, 8, 8, 3, 4, 0, 0)
FIRST_AHEAD = (1, 3, 6)
PACES = (PACE_AHEAD, PACE_BEHIND)
AFTER_START = tuple(told for told in AFTER_START if PACES[told[2]][told[1]])
AT_FORWARD = tuple(told for told in AT_FORWARD if PACES[told[2]][told[1]])
AT_BACKWARD = tuple(told for told in AT_BACKWARD if PACES[told[2]][told[1]])
TOLD = AFTER_START + AT_FORWARD + AT_BACKWARD
GREETS = tuple(sorted({(min(i, j), max(i, j)) for i, j, _ in TOLD if abs(i - j) > 1}))


def any_of(place, places):
    found = place < 0
    for one in places:
        found = jnp.logical_or(found, place == one)
    return found


def dot(operand, weights):
    return lax.dot_general(operand, weights, NN, preferred_element_type=F32)


def gathered(vector, cols, row, count):
    return jnp.concatenate([vector[cols[k, row]] for k in range(count)], axis=1)


def row_apply(blocks, vector, cols, row):
    return dot(gathered(vector, cols, row, KH), blocks[row].reshape(KH * BLK, BLK))


def transpose_factor(blocks):
    def one(row, carry):
        for k in range(KH):
            blocks[row, k] = blocks[row, k].T
        return carry

    lax.fori_loop(0, HALF, one, 0, unroll=2)


def split_couplings(raw, diagonal, beside, base):
    def one(row, carry):
        diagonal[row] = raw[row, 0].T
        beside[base + row] = raw[row, 1].T
        return carry

    lax.fori_loop(0, HALF, one, 0, unroll=4)


def sweep_kernel(
    sources_hbm, frontal, couplings, pattern, cols, swept,
    sources, partial, theirs_part, factor, raw, diag_ahead, diag_behind, side_ahead, side_behind, diag_next, diag_prior,
    rounded, source_next, their_pattern, their_cols, field, incoming, later, incoming_plus, later_plus, reduced, pulled, out_fwd, out_bwd,
    load_sem, once_send, once_recv, fwd_send, fwd_recv, bwd_send, bwd_recv, go,
):
    depth = lax.axis_index("depth")
    half = lax.axis_index("lat")
    place = lax.rem(depth, SEG)
    other = 1 - half
    base = half * HALF
    their_base = other * HALF

    load_factor = pltpu.make_async_copy(frontal, factor, load_sem.at[0])
    load_ahead = pltpu.make_async_copy(couplings.at[0], raw.at[0], load_sem.at[1])
    load_behind = pltpu.make_async_copy(couplings.at[1], raw.at[1], load_sem.at[2])
    load_sources = pltpu.make_async_copy(sources_hbm, sources, load_sem.at[4])
    load_sources.start()
    load_ahead.start()
    load_factor.start()
    load_behind.start()

    barrier = pltpu.get_barrier_semaphore()

    def greet(depth_index, lat):
        pl.semaphore_signal(barrier, inc=1, device_id=(depth_index, lat), device_id_type=MESH)

    greet(depth, other)

    @pl.when(place > 0)
    def _():
        greet(depth - 1, half)
        greet(depth - 1, other)

    @pl.when(place < SEG - 1)
    def _():
        greet(depth + 1, half)
        greet(depth + 1, other)

    for one, two in GREETS:
        @pl.when(place == one)
        def _():
            greet(depth + (two - one), half)

        @pl.when(place == two)
        def _():
            greet(depth - (two - one), half)

    at_edge = jnp.logical_or(place == 0, place == SEG - 1)
    callers = jnp.where(at_edge, 3, 5)
    for pair in GREETS:
        callers = callers + jnp.where(any_of(place, pair), 1, 0)

    load_sources.wait()
    load_ahead.wait()

    @pl.when(place == 0)
    def _():
        for row in range(HALF):
            reduced[base + row] = sources[:, row * BLK:(row + 1) * BLK].astype(BF16)

    @pl.when(place > 0)
    def _():
        split_couplings(raw.at[0], diag_ahead, side_ahead, base)
        for row in range(HALF):
            rounded[row] = sources[:, row * BLK:(row + 1) * BLK].astype(BF16)

    pl.semaphore_wait(barrier, callers)

    def tell(table):
        for one, two, slot in table:
            @pl.when(place == one)
            def _():
                pl.semaphore_signal(
                    go.at[slot], inc=1, device_id=(depth + (two - one), half), device_id_type=MESH
                )

    def wait_told(slot, among):
        places = [two for _, two, kind in TOLD if kind == slot and two in among]

        @pl.when(any_of(place, places))
        def _():
            pl.semaphore_wait(go.at[slot], 1)

    def once(source, target, slot, step, lat):
        return pltpu.make_async_remote_copy(
            src_ref=source, dst_ref=target, send_sem=once_send.at[slot], recv_sem=once_recv.at[slot],
            device_id=(depth + step, lat), device_id_type=MESH,
        )

    mine = pl.ds(base, HALF)
    theirs = pl.ds(their_base, HALF)
    swaps_ahead = any_of(place, SWAP_AHEAD)
    swaps_behind = any_of(place, SWAP_BEHIND)
    ahead_swaps = any_of(place + 1, SWAP_AHEAD)
    behind_swaps = any_of(place - 1, SWAP_BEHIND)
    give_reduced = once(reduced.at[mine], reduced.at[mine], 0, 0, other)
    take_reduced = once(reduced.at[theirs], reduced.at[theirs], 0, 0, other)
    give_pulled = once(pulled.at[mine], pulled.at[mine], 7, 0, other)
    take_pulled = once(pulled.at[theirs], pulled.at[theirs], 7, 0, other)
    give_pattern = once(pattern, their_pattern, 1, 0, other)
    give_source = once(rounded, source_next, 2, -1, half)
    give_diag_ahead = once(diag_ahead, diag_next, 3, -1, half)
    give_diag_behind = once(diag_behind, diag_prior, 4, 1, half)

    def side_copy(blocks, kind, owner, first, rows):
        part = blocks.at[pl.ds(owner * HALF + first, rows)]
        return once(part, part, 5 + kind, 0, other)

    def give_side(blocks, kind, paces, places):
        for pace in sorted(set(paces[p] for p in places if paces[p])):
            group = [p for p in places if paces[p] == pace]

            @pl.when(any_of(place, group))
            def _():
                wait_told(kind, group)

                def part(step, carry):
                    copy = side_copy(blocks, kind, half, step * pace, pace)
                    copy.start()
                    copy.wait_send()
                    return carry

                lax.fori_loop(0, HALF // pace, part, 0)

    def take_side(blocks, kind):
        side_copy(blocks, kind, other, 0, HALF).wait_recv()

    def chunk_copy(source, target, chunk, kind, owner, step, send, recv):
        return pltpu.make_async_remote_copy(
            src_ref=source.at[kind // 2, pl.ds(chunk * ROWS, ROWS)],
            dst_ref=target.at[pl.ds(owner * HALF + chunk * ROWS, ROWS)],
            send_sem=send.at[kind, chunk], recv_sem=recv.at[kind, chunk],
            device_id=(depth + step, other if kind else half), device_id_type=MESH,
        )

    def forward_copy(chunk, kind, owner):
        return chunk_copy(out_fwd, incoming_plus if kind == 2 else incoming, chunk, kind, owner, 1, fwd_send, fwd_recv)

    def backward_copy(chunk, kind, owner):
        return chunk_copy(out_bwd, later_plus if kind == 2 else later, chunk, kind, owner, -1, bwd_send, bwd_recv)

    def wait_arrivals(make, kinds):
        for kind in kinds:
            for chunk in range(CHUNKS):
                make(chunk, kind, other if kind else half).wait_recv()

    def wait_sent(make, swaps):
        for kind in (0, 1):
            for chunk in range(CHUNKS):
                make(chunk, kind, half).wait_send()

        @pl.when(jnp.logical_not(swaps))
        def _():
            for chunk in range(CHUNKS):
                make(chunk, 2, half).wait_send()

    def in_chunks(make, out, compute, ahead_of, swaps):
        for chunk in range(CHUNKS + 1):
            if chunk < CHUNKS:
                for row in range(chunk * ROWS, (chunk + 1) * ROWS):
                    out[0, row] = compute(row).astype(BF16)
                make(chunk, 1, half).start()
                make(chunk, 0, half).start()
            if chunk > 0:
                for row in range((chunk - 1) * ROWS, chunk * ROWS):
                    out[1, row] = ahead_of(out[0, row], row).astype(BF16)

                @pl.when(jnp.logical_not(swaps))
                def _():
                    make(chunk - 1, 2, half).start()

    def next_source(sent, row):
        return source_next[row] - dot(sent, diag_next[row])

    def prior_pulled(sent, row):
        return dot(sent, diag_prior[row])

    @pl.when(place == 0)
    def _():
        give_reduced.start()
        give_reduced.wait_send()

    tell(AFTER_START)
    give_pattern.start()

    @pl.when(jnp.logical_and(place > 0, jnp.logical_not(swaps_ahead)))
    def _():
        give_source.start()
        give_diag_ahead.start()

    give_side(side_ahead, AHEAD, PACE_AHEAD, FIRST_AHEAD)

    load_behind.wait()

    def take_diag_prior():
        @pl.when(jnp.logical_not(behind_swaps))
        def _():
            give_diag_behind.wait_recv()

    def prepare_behind():
        split_couplings(raw.at[1], diag_behind, side_behind, base)

    def start_diag_behind():
        @pl.when(jnp.logical_not(swaps_behind))
        def _():
            give_diag_behind.start()

    @pl.when(place < SEG - 1)
    def _():
        prepare_behind()

        @pl.when(lax.rem(place, 2) == 0)
        def _():
            start_diag_behind()

    load_factor.wait()
    transpose_factor(factor)

    give_side(side_ahead, AHEAD, PACE_AHEAD, [p for p in range(1, SEG) if p not in FIRST_AHEAD])
    give_pattern.wait_recv()
    load_cols = pltpu.make_async_copy(their_pattern, their_cols, load_sem.at[3])
    load_cols.start()
    load_cols.wait()

    @pl.when(place == 0)
    def _():
        take_reduced.wait_recv()

    def forward_row(row):
        value = row_apply(factor, reduced, cols, row)
        field[row] = value
        return value

    def last_row(row):
        value = row_apply(factor, reduced, cols, row)
        swept[:, row * BLK:(row + 1) * BLK] = value
        return value

    def backward_row(row):
        value = field[row] - row_apply(factor, pulled, cols, row)
        swept[:, row * BLK:(row + 1) * BLK] = value
        return value

    @pl.when(place > 0)
    def _():
        wait_arrivals(forward_copy, (0,))
        for row in range(HALF):
            near = dot(incoming[base + row], diag_ahead[row])
            partial[row] = sources[:, row * BLK:(row + 1) * BLK] - near
        wait_arrivals(forward_copy, (1,))
        for row in range(HALF):
            beside = dot(incoming[cols[1, row]], side_ahead[base + row])
            reduced[base + row] = (partial[row] - beside).astype(BF16)

        @pl.when(swaps_ahead)
        def _():
            give_reduced.start()
            take_reduced.wait_recv()

        @pl.when(jnp.logical_not(swaps_ahead))
        def _():
            take_side(side_ahead, AHEAD)
            for row in range(HALF):
                theirs_part[row] = dot(incoming[their_cols[1, row]], side_ahead[their_base + row])
            wait_arrivals(forward_copy, (2,))
            for row in range(HALF):
                reduced[their_base + row] = (incoming_plus[their_base + row] - theirs_part[row]).astype(BF16)

    @pl.when(jnp.logical_and(place < SEG - 1, jnp.logical_not(ahead_swaps)))
    def _():
        give_source.wait_recv()
        give_diag_ahead.wait_recv()

    @pl.when(place == SEG - 1)
    def _():
        take_diag_prior()
        in_chunks(backward_copy, out_bwd, last_row, prior_pulled, behind_swaps)

    @pl.when(place < SEG - 1)
    def _():
        in_chunks(forward_copy, out_fwd, forward_row, next_source, ahead_swaps)

    tell(AT_FORWARD)

    @pl.when(place < SEG - 1)
    def _():
        wait_sent(forward_copy, ahead_swaps)

        @pl.when(lax.rem(place, 2) == 1)
        def _():
            start_diag_behind()

    give_side(side_behind, BEHIND, PACE_BEHIND, range(SEG - 1))

    @pl.when(place < SEG - 1)
    def _():
        wait_arrivals(backward_copy, (0,))
        for row in range(HALF):
            partial[row] = dot(later[base + row], diag_behind[row])
        wait_arrivals(backward_copy, (1,))
        for row in range(HALF):
            beside = dot(later[cols[1, row]], side_behind[base + row])
            pulled[base + row] = (partial[row] + beside).astype(BF16)

        @pl.when(swaps_behind)
        def _():
            give_pulled.start()
            take_pulled.wait_recv()

        @pl.when(jnp.logical_not(swaps_behind))
        def _():
            take_side(side_behind, BEHIND)
            for row in range(HALF):
                theirs_part[row] = dot(later[their_cols[1, row]], side_behind[their_base + row])
            wait_arrivals(backward_copy, (2,))
            for row in range(HALF):
                pulled[their_base + row] = (later_plus[their_base + row] + theirs_part[row]).astype(BF16)

        @pl.when(place > 0)
        def _():
            take_diag_prior()
            in_chunks(backward_copy, out_bwd, backward_row, prior_pulled, behind_swaps)

        @pl.when(place == 0)
        def _():
            for row in range(HALF):
                backward_row(row)


    tell(AT_BACKWARD)

    @pl.when(place > 0)
    def _():
        wait_sent(backward_copy, behind_swaps)

    @pl.when(swaps_ahead)
    def _():
        give_reduced.wait_send()

    @pl.when(swaps_behind)
    def _():
        give_pulled.wait_send()

    give_pattern.wait_send()

    @pl.when(jnp.logical_and(place > 0, jnp.logical_not(swaps_ahead)))
    def _():
        give_source.wait_send()
        give_diag_ahead.wait_send()

    @pl.when(jnp.logical_and(place < SEG - 1, jnp.logical_not(swaps_behind)))
    def _():
        give_diag_behind.wait_send()


def local(sources, frontal, couplings, pattern):
    vector = pltpu.VMEM((NBR, SHOTS, BLK), BF16)
    half_vector = pltpu.VMEM((HALF, SHOTS, BLK), BF16)
    half_double = pltpu.VMEM((2, HALF, SHOTS, BLK), BF16)
    half_blocks = pltpu.VMEM((HALF, BLK, BLK), BF16)
    blocks = pltpu.VMEM((NBR, BLK, BLK), BF16)
    vmem = pl.BlockSpec(memory_space=pltpu.VMEM)
    hbm = pl.BlockSpec(memory_space=pl.ANY)
    smem = pl.BlockSpec(memory_space=pltpu.SMEM)
    chunk_sem = pltpu.SemaphoreType.DMA((3, CHUNKS))
    columns = pattern[0].T
    once_sem = pltpu.SemaphoreType.DMA((8,))
    out = pl.pallas_call(
        sweep_kernel,
        out_shape=jax.ShapeDtypeStruct((SHOTS, HALF * BLK), F32),
        in_specs=[hbm, hbm, hbm, hbm, smem],
        out_specs=vmem,
        scratch_shapes=[
            pltpu.VMEM((SHOTS, HALF * BLK), F32),
            pltpu.VMEM((HALF, SHOTS, BLK), F32),
            pltpu.VMEM((HALF, SHOTS, BLK), F32),
            pltpu.VMEM((HALF, KH, BLK, BLK), BF16),
            pltpu.VMEM((2, HALF, KC, BLK, BLK), BF16),
            half_blocks, half_blocks, blocks, blocks, half_blocks, half_blocks,
            half_vector, half_vector,
            pltpu.VMEM((KH, HALF), jnp.int32),
            pltpu.SMEM((KH, HALF), jnp.int32),
            pltpu.VMEM((HALF, SHOTS, BLK), F32),
            vector, vector, vector, vector, vector, vector, half_double, half_double,
            pltpu.SemaphoreType.DMA((5,)),
            once_sem, once_sem, chunk_sem, chunk_sem, chunk_sem, chunk_sem,
            pltpu.SemaphoreType.REGULAR((2,)),
        ],
        compiler_params=pltpu.CompilerParams(
            collective_id=0, has_side_effects=True, vmem_limit_bytes=60 * 1024 * 1024
        ),
    )(sources[0], frontal[0], couplings[0], columns, columns)
    return out[None]


def solution(mesh):
    return jax.shard_map(
        local,
        mesh=mesh,
        in_specs=(
            P("depth", None, "lat"),
            P("depth", "lat", None, None, None),
            P("depth", None, "lat", None, None, None),
            P("depth", "lat", None),
        ),
        out_specs=P("depth", None, "lat"),
        check_vma=False,
    )
```
